256 devices in a mesh: filt: 8 (over z_hi, core), space: 32 (over y, x, z_lo).
Axes of the slice: x: 4, y: 4, z: 8 (z_hi: 4, z_lo: 2; z = z_hi * 2 + z_lo), core: 2. Of those that a mesh axis runs over, the one named last changes fastest.
Arguments:
- activation: bfloat16 [32, 64, 128, 256], P(None, 'space', 'filt'), may hold values from -6 to 6
- preact: bfloat16 [32, 64, 128, 256], P(None, 'space', 'filt'), may hold values from -6 to 6
- grad_out: bfloat16 [64, 32, 64, 128], P('filt', 'space'), may hold values from -6 to 6
- weight_a: bfloat16 [27, 32, 32], replicated, may hold values from -0.21875 to 0.21875
- weight_b: bfloat16 [27, 64, 32], P(None, 'filt'), may hold values from -0.625 to 0.625
Outputs:
- grad_input: bfloat16 [32, 64, 128, 256], P(None, 'space', 'filt')
- grad_wa: float32 [27, 32, 32], replicated
- grad_wb: float32 [27, 64, 32], P(None, 'filt')
The draws below stay inside these ranges and needn't reach their ends.
All inputs are finite; a program needn't handle non-finite values.
Results may differ from the reference program's by a relative error of at most 0.0049.
Values may be sent and summed in bfloat16 or wider, within the bound.
A program may use at most 128 MiB of HBM per device.

```python
import math
import jax
import jax.numpy as jnp
from jax import lax

CA = 32
CB = 64
NZB = 128
NXB = 32
NYB = 64
NXA = 64
NYA = 128
NZA = 256


def block_levels(own_key, shape, pieces, low, top_value):
    factor_of, own = 1.0, jax.random.fold_in(own_key, 6)
    for axis_at, parts in pieces:
        draws = jnp.exp(jax.random.uniform(jax.random.fold_in(own, axis_at), (parts,), jnp.float32, low / len(pieces), top_value / len(pieces)))
        factor_of = factor_of * jnp.repeat(draws, shape[axis_at] // parts).reshape([-1 if axis == axis_at else 1 for axis in range(len(shape))])
    return factor_of


def noise(own_key, extent, deviation, most, split=(), held_as=jnp.bfloat16):
    gain = block_levels(own_key, extent, split, -0.22, 0.18) if split else 1.0
    drawn = jax.random.normal(own_key, extent, jnp.float32) * deviation * gain
    return jnp.minimum(jnp.maximum(drawn, -most), most).astype(held_as)


def setup_inputs(seed: int = 0) -> dict:
    key_of = jax.random.split(jax.random.key(seed), 6)
    activation = noise(key_of[0], (CA, NXA, NYA, NZA), 1.0, 6.0, ((1, 32), (2, 8)))
    preact = noise(key_of[1], (CA, NXA, NYA, NZA), 1.0, 6.0, ((1, 32), (2, 8)))
    grad_out = noise(key_of[2], (CB, NXB, NYB, NZB), 1.0, 6.0, ((0, 8), (1, 32)))
    weight_a = noise(key_of[3], (27, CA, CA), (27 * CA) ** -0.5, 0.21875)
    weight_b = noise(key_of[4], (27, CB, CA), (27 * CB // 16) ** -0.5, 0.625, ((1, 8),))
    return dict(activation=activation, preact=preact, grad_out=grad_out, weight_a=weight_a, weight_b=weight_b)


def tap_list():
    result = []
    for dx in (-1, 0, 1):
        for dy in (-1, 0, 1):
            for dz in (-1, 0, 1):
                result.append((1 - dx, 1 - dy, 1 - dz))
    return result

def padded_field(field):
    return jnp.pad(field.astype(jnp.float32), ((0, 0), (1, 1), (1, 1), (1, 1)))

def input_grad(padded, weight, shape):
    total = jnp.zeros((weight.shape[2],) + shape, jnp.float32)
    wide = weight.astype(jnp.float32)
    for index, start in enumerate(tap_list()):
        piece = padded[:, start[0]:start[0] + shape[0], start[1]:start[1] + shape[1], start[2]:start[2] + shape[2]]
        total = total + jnp.einsum('oi,oxyz->ixyz', wide[index], piece)
    return total

def weight_grad(padded, field):
    shape = field.shape[1:]
    wide = field.astype(jnp.float32)
    terms = []
    for start in tap_list():
        piece = padded[:, start[0]:start[0] + shape[0], start[1]:start[1] + shape[1], start[2]:start[2] + shape[2]]
        terms.append(jnp.einsum('oxyz,ixyz->oi', piece, wide))
    return jnp.stack(terms)

def reference(activation, preact, grad_out, weight_a, weight_b):
    fine = preact.astype(jnp.float32)
    chans, sx, sy, sz = fine.shape
    blocks = jnp.maximum(fine, 0.0).reshape(chans, sx // 2, 2, sy // 2, 2, sz // 2, 2)
    pooled = lax.optimization_barrier(jnp.mean(blocks, axis=(2, 4, 6))).astype(jnp.bfloat16)
    coarse_shape = grad_out.shape[1:]
    padded_out = padded_field(grad_out)
    grad_pooled = input_grad(padded_out, weight_b, coarse_shape).astype(jnp.bfloat16)
    scale_b = 1.0 / math.sqrt(coarse_shape[0] * coarse_shape[1] * coarse_shape[2])
    grad_wb = weight_grad(padded_out, pooled) * scale_b
    wide = grad_pooled.astype(jnp.float32)
    cx, cy, cz = coarse_shape
    upsampled = jnp.broadcast_to(wide[:, :, None, :, None, :, None], (chans, cx, 2, cy, 2, cz, 2)).reshape(chans, sx, sy, sz)
    grad_pre = jnp.where(fine > 0.0, upsampled * 0.125, 0.0).astype(jnp.bfloat16)
    padded_pre = padded_field(grad_pre)
    grad_input = input_grad(padded_pre, weight_a, (sx, sy, sz)).astype(jnp.bfloat16)
    scale_a = 1.0 / math.sqrt(sx * sy * sz)
    grad_wa = weight_grad(padded_pre, activation) * scale_a
    return (grad_input, grad_wa, grad_wb)
```

```python
import math

import jax
import jax.numpy as jnp
from jax import lax
from jax.experimental import pallas as pl
from jax.experimental.pallas import tpu as pltpu
from jax.sharding import PartitionSpec as P

BF = jnp.bfloat16
F32 = jnp.float32
NF = 8
ROWS = 8
NXY = 16


def shifted(values, step):
    width = values.shape[-1]
    axis = values.ndim - 1
    lane = lax.broadcasted_iota(jnp.int32, values.shape, axis)
    rolled = pltpu.roll(values, step % width, axis)
    edge = 0 if step == 1 else width - 1
    return jnp.where(lane == edge, 0.0, rolled)


def kernel(
    gout,
    pre,
    act,
    wa0,
    wb0,
    up,
    down,
    out,
    gwa_out,
    gwb_out,
    grid_b,
    wb_all,
    tb,
    ta,
    prh,
    gpc,
    gp,
    act3,
    racc,
    gwb,
    rb1,
    rb2,
    sb,
    fin,
    gwa,
    ra1,
    ra2,
    ra3,
    sa,
    s1,
    r1,
    sw,
    rw,
    sp,
    rp,
    sc,
    rc,
    sb1,
    qb1,
    sb2,
    qb2,
    sb3,
    qb3,
    sa1,
    qa1,
    sa2,
    qa2,
    sa3,
    qa3,
):
    f = lax.axis_index("filt")
    p = lax.axis_index("space")
    ns = lax.axis_size("space")
    xy = p // 2
    zl = p % 2

    def fmod(v):
        return lax.rem(v + NF, NF)

    def smod(v):
        return lax.rem(v + ns, ns)

    def xymod(v):
        return lax.rem(v + NXY, NXY)

    def send(src, dst, ss, rs, tf, tp):
        pltpu.make_async_remote_copy(
            src_ref=src,
            dst_ref=dst,
            send_sem=ss,
            recv_sem=rs,
            device_id={"filt": tf, "space": tp},
            device_id_type=pl.DeviceIdType.MESH,
        ).start()

    def wait(ref, sem):
        pltpu.make_async_copy(ref, ref, sem).wait()

    barrier = pltpu.get_barrier_semaphore()

    def greet(tf, tp):
        pl.semaphore_signal(
            barrier,
            inc=1,
            device_id={"filt": tf, "space": tp},
            device_id_type=pl.DeviceIdType.MESH,
        )

    @pl.loop(0, NF)
    def _(j):
        greet(fmod(f + j), smod(p - 1))
        greet(fmod(f + j), smod(p + 1))

    @pl.loop(1, NF)
    def _(j):
        greet(fmod(f + j), p)

    @pl.loop(1, NXY)
    def _(j):
        greet(f, xymod(xy + j) * 2 + zl)

    @pl.loop(0, NF)
    def _(j):
        greet(fmod(f + j), xy * 2 + 1 - zl)

    pl.semaphore_wait(barrier, 3 * NF - 1 + NXY - 1 + NF)

    def block(tf):
        return gout.at[pl.ds(pl.multiple_of(tf * (ROWS * 8), 16), (ROWS + 2) * 8)]

    @pl.loop(1, NF)
    def _(j):
        tf = fmod(f + j)
        send(wb0, wb_all.at[f], sw.at[j], rw.at[f], tf, p)
        send(block(tf), grid_b.at[f, 1], s1.at[1, j], r1.at[1, f], tf, p)

    @pl.loop(0, NF)
    def _(j):
        tf = fmod(f + j)
        send(block(tf), grid_b.at[f, 2], s1.at[0, j], r1.at[2, f], tf, smod(p - 1))
        send(block(tf), grid_b.at[f, 0], s1.at[2, j], r1.at[0, f], tf, smod(p + 1))

    pre_moves = (
        (pre.at[0], prh.at[3, pl.ds(1, 16)], 0, -1),
        (pre.at[1], prh.at[0, pl.ds(1, 16)], 0, 1),
        (pre.at[pl.ds(0, 2), 0], prh.at[pl.ds(1, 2), 17], -1, 0),
        (pre.at[pl.ds(0, 2), 15], prh.at[pl.ds(1, 2), 0], 1, 0),
        (pre.at[0, 0], prh.at[3, 17], -1, -1),
        (pre.at[0, 15], prh.at[3, 0], 1, -1),
        (pre.at[1, 0], prh.at[0, 17], -1, 1),
        (pre.at[1, 15], prh.at[0, 0], 1, 1),
    )
    for n, (src, dst, df, dp) in enumerate(pre_moves):
        send(src, dst, sp.at[n], rp.at[n], fmod(f + df), smod(p + dp))

    own = block(f)
    grid_b[f, 1] = own[...]
    grid_b[:, 3] = jnp.zeros((NF,) + grid_b.shape[2:], BF)
    wb_all[f] = wb0[...]
    prh[1:3, 1:17] = pre[...]

    wide_a = wa0[...].astype(F32)
    for n, turn in enumerate((0, 32, 128, 160)):
        ta[n * 96 : n * 96 + 96] = (
            pltpu.roll(wide_a, turn, 1) if turn else wide_a
        ).astype(BF)

    relu = jnp.maximum(pre[...], jnp.zeros((), BF)).reshape(2, ROWS, 2, 32, 256)
    total = jnp.zeros((ROWS * 32, 128), F32)
    for x2 in range(2):
        for y2 in range(2):
            total += jnp.dot(
                relu[x2, :, y2].reshape(ROWS * 32, 256),
                down[...],
                preferred_element_type=F32,
            )
    pooled = (total * 0.125).astype(BF).astype(F32)
    pooled3 = jnp.stack(
        [
            shifted(pooled, 1).astype(BF).reshape(ROWS // 2, 2, 32, 128),
            pooled.astype(BF).reshape(ROWS // 2, 2, 32, 128),
            shifted(pooled, -1).astype(BF).reshape(ROWS // 2, 2, 32, 128),
            jnp.zeros((ROWS // 2, 2, 32, 128), BF),
        ],
        axis=2,
    ).reshape(ROWS // 2, 256, 128)
    pooled_cat = jnp.concatenate([pooled3[b] for b in range(ROWS // 2)], axis=1)

    @pl.loop(0, 8)
    def _(b):
        for x2 in range(2):
            for y2 in range(2):
                slab = act[x2, 2 * b + y2]
                wide = slab.astype(F32)
                base = (x2 * 2 + y2) * 128
                act3[b, base : base + 32] = shifted(wide, 1).astype(BF)
                act3[b, base + 32 : base + 64] = slab
                act3[b, base + 64 : base + 96] = shifted(wide, -1).astype(BF)
                act3[b, base + 96 : base + 128] = jnp.zeros((32, 256), BF)

    racc[...] = jnp.zeros(racc.shape, F32)

    @pl.loop(1, NF)
    def _(j):
        wait(wb_all.at[0], rw.at[fmod(f + j)])

    for n in range(NF):
        wide_b = wb_all[n].astype(F32)
        tb[0:96, n * 128 : n * 128 + 128] = wb_all[n]
        tb[96:192, n * 128 : n * 128 + 128] = pltpu.roll(wide_b, 8, 1).astype(BF)

    @pl.loop(1, NF)
    def _(j):
        wait(grid_b.at[0, 0], r1.at[1, fmod(f + j)])

    @pl.loop(0, NF)
    def _(j):
        wait(grid_b.at[0, 0], r1.at[0, j])
        wait(grid_b.at[0, 0], r1.at[2, j])

    @pl.when(p == 0)
    def _():
        grid_b[:, 0] = jnp.zeros((NF,) + grid_b.shape[2:], BF)

    @pl.when(p == ns - 1)
    def _():
        grid_b[:, 2] = jnp.zeros((NF,) + grid_b.shape[2:], BF)

    g_cat = jnp.concatenate(
        [grid_b[:, :, 16 * b : 16 * b + 32, :].reshape(1024, 128) for b in range(ROWS // 2)],
        axis=1,
    )
    prod = jnp.dot(tb[...], g_cat, preferred_element_type=F32)
    for b in range(ROWS // 2):
        part = prod[:, b * 128 : b * 128 + 128].reshape(2, 3, 32, 128)
        rows = part[:, 1] + shifted(part[:, 0], -1) + shifted(part[:, 2], 1)
        gpc[1, 1 + 2 * b : 3 + 2 * b] = rows.astype(BF)

    coarse_moves = (
        (gpc.at[1, pl.ds(1, ROWS)], gpc.at[2, pl.ds(1, ROWS)], 0, -1),
        (gpc.at[1, pl.ds(1, ROWS)], gpc.at[0, pl.ds(1, ROWS)], 0, 1),
        (gpc.at[1, 1], gpc.at[1, ROWS + 1], -1, 0),
        (gpc.at[1, ROWS], gpc.at[1, 0], 1, 0),
        (gpc.at[1, 1], gpc.at[2, ROWS + 1], -1, -1),
        (gpc.at[1, ROWS], gpc.at[2, 0], 1, -1),
        (gpc.at[1, 1], gpc.at[0, ROWS + 1], -1, 1),
        (gpc.at[1, ROWS], gpc.at[0, 0], 1, 1),
    )
    for n, (src, dst, df, dp) in enumerate(coarse_moves):
        send(src, dst, sc.at[n], rc.at[n], fmod(f + df), smod(p + dp))

    pairs = lax.dot_general(
        g_cat, pooled_cat, (((1,), (1,)), ((), ())), preferred_element_type=F32
    ).reshape(NF, 4, 4, 8, 256)
    folded = pairs[:, :3, :3, :, :128] + pairs[:, :3, 1:, :, 128:]
    folded = jnp.concatenate(
        [folded.reshape(NF, 72, 128), jnp.zeros((NF, 24, 128), F32)], axis=1
    )
    gwb[...] = folded.astype(BF).reshape(2 * NF, 48, 128)

    @pl.loop(1, NXY)
    def _(j):
        k = xymod(xy + j)
        send(gwb.at[k], rb1.at[xy], sb1.at[j], qb1.at[xy], f, k * 2 + zl)

    rb1[xy] = gwb[xy]

    for n, (src, dst, df, dp) in enumerate(coarse_moves):
        wait(dst, rc.at[n])
    for n, (src, dst, df, dp) in enumerate(pre_moves):
        wait(dst, rp.at[n])

    @pl.when(p == 0)
    def _():
        prh[0] = jnp.zeros(prh.shape[1:], BF)

    @pl.when(p == ns - 1)
    def _():
        prh[3] = jnp.zeros(prh.shape[1:], BF)

    @pl.when(f == 0)
    def _():
        prh[:, 0] = jnp.zeros((4, 32, 256), BF)

    @pl.when(f == NF - 1)
    def _():
        prh[:, 17] = jnp.zeros((4, 32, 256), BF)

    for plane in range(3):
        fine = (
            jnp.dot(gpc[plane].reshape(320, 128), up[...], preferred_element_type=F32)
            .astype(BF)
            .reshape(10, 32, 256)
        )
        for xh in ((0,), (1, 2), (3,))[plane]:
            for row in range(10):
                for yh in (2 * row - 1, 2 * row):
                    if 0 <= yh <= 17:
                        gp[xh, yh] = jnp.where(
                            prh[xh, yh] > jnp.zeros((), BF), fine[row], jnp.zeros((), BF)
                        )

    @pl.loop(0, 8)
    def _(b):
        cells = gp[:, pl.ds(2 * b, 4)].reshape(512, 256)
        part = jnp.dot(ta[...], cells, preferred_element_type=F32).reshape(2, 2, 3, 32, 256)
        rows = part[:, :, 1] + shifted(part[:, :, 0], -1) + shifted(part[:, :, 2], 1)
        out[:, pl.ds(2 * b, 2)] = rows.astype(BF)
        racc[...] += lax.dot_general(
            cells, act3[b], (((1,), (1,)), ((), ())), preferred_element_type=F32
        )

    taps = []
    for dx in range(3):
        for dy in range(3):
            term = None
            for x2 in range(2):
                for y2 in range(2):
                    r0 = ((x2 + dx) * 4 + y2 + dy) * 32
                    c0 = (x2 * 2 + y2) * 128
                    piece = racc[r0 : r0 + 32, c0 : c0 + 128]
                    term = piece if term is None else term + piece
            taps.append(term)
    full = jnp.concatenate(taps, axis=0)
    rest = full[216:288]
    tail = jnp.concatenate([pltpu.roll(rest, turn, 1) for turn in (96, 64, 32)], axis=0)
    lane = lax.broadcasted_iota(jnp.int32, (216, 128), 1)
    packed = jnp.where(lane < 96, full[:216], tail)
    packed = jnp.concatenate([packed, jnp.zeros((40, 128), F32)], axis=0)
    gwa[...] = packed.astype(BF).reshape(NXY, 16, 128)

    @pl.loop(1, NXY)
    def _(j):
        k = xymod(xy + j)
        send(gwa.at[k], ra1.at[xy], sa1.at[j], qa1.at[xy], f, k * 2 + zl)

    ra1[xy] = gwa[xy]

    @pl.loop(1, NXY)
    def _(j):
        wait(rb1.at[0], qb1.at[xymod(xy + j)])

    owner = xy // 2
    me2 = f * 2 + zl
    sb[...] = jnp.sum(rb1[...].astype(F32), axis=0).astype(BF)
    for zt in range(2):

        @pl.when((f != owner) | (zl != zt))
        def _():
            send(sb, rb2.at[me2], sb2.at[zt], qb2.at[me2], owner, xy * 2 + zt)

    @pl.loop(1, NXY)
    def _(j):
        wait(ra1.at[0], qa1.at[xymod(xy + j)])

    sa[...] = jnp.sum(ra1[...].astype(F32), axis=0).astype(BF)

    @pl.loop(1, NXY)
    def _(j):
        t = xymod(me2 + j)
        send(sa, ra2.at[me2], sa2.at[j], qa2.at[me2], t // 2, xy * 2 + lax.rem(t, 2))

    ra2[me2] = sa[...]

    half = lax.rem(xy, 2)

    @pl.when(f == owner)
    def _():
        rb2[me2] = sb[...]

        @pl.loop(1, NXY)
        def _(j):
            wait(rb2.at[0], qb2.at[xymod(me2 + j)])

        fin[half] = jnp.sum(rb2[...].astype(F32), axis=0)

        @pl.loop(1, NXY)
        def _(j):
            send(fin.at[half], fin.at[half], sb3.at[j], qb3.at[half], f, xymod(xy + j) * 2 + zl)

    @pl.loop(1, NXY)
    def _(j):
        wait(ra2.at[0], qa2.at[xymod(me2 + j)])

    ra3[xy] = jnp.sum(ra2[...].astype(F32), axis=0).astype(BF)

    @pl.loop(1, NXY)
    def _(j):
        k = xymod(xy + j)
        send(ra3.at[xy], ra3.at[xy], sa3.at[j], qa3.at[xy], f, k * 2 + zl)

    for h in range(2):

        @pl.when(xy != 2 * f + h)
        def _():
            wait(fin.at[h], qb3.at[h])

        gwb_out[h] = fin[h] * (1.0 / math.sqrt(ns * NF * ROWS * 128))

    @pl.loop(1, NXY)
    def _(j):
        wait(ra3.at[0], qa3.at[xymod(xy + j)])

    gwa_out[...] = ra3[...].astype(F32) * (1.0 / math.sqrt(8 * ns * NF * ROWS * 128))

    @pl.loop(1, NF)
    def _(j):
        wait(wb0, sw.at[j])
        wait(grid_b.at[0, 0], s1.at[1, j])

    @pl.loop(0, NF)
    def _(j):
        wait(grid_b.at[0, 0], s1.at[0, j])
        wait(grid_b.at[0, 0], s1.at[2, j])

    for n, (src, dst, df, dp) in enumerate(pre_moves):
        wait(src, sp.at[n])
    for n, (src, dst, df, dp) in enumerate(coarse_moves):
        wait(src, sc.at[n])

    @pl.loop(1, NXY)
    def _(j):
        wait(gwb.at[0], sb1.at[j])
        wait(gwa.at[0], sa1.at[j])
        wait(sa, sa2.at[j])
        wait(ra3.at[0], sa3.at[j])

    for zt in range(2):

        @pl.when((f != owner) | (zl != zt))
        def _():
            wait(sb, sb2.at[zt])

    @pl.when(f == owner)
    def _():
        @pl.loop(1, NXY)
        def _(j):
            wait(fin.at[0], sb3.at[j])


def tap_rows(weight):
    o, i = weight.shape[1:]
    parts = weight.reshape(3, 3, 3, o, i)[::-1, ::-1]
    parts = jnp.transpose(parts, (2, 4, 0, 1, 3))
    parts = jnp.pad(parts, ((0, 0), (0, 0), (0, 1), (0, 1), (0, 0)))
    return parts.reshape(3 * i, 16 * o)


def per_device(activation, preact, grad_out, weight_a, weight_b):
    depth = grad_out.shape[3]
    gout = jnp.pad(jnp.transpose(grad_out[:, 0], (1, 0, 2)), ((1, 1), (0, 0), (0, 0)))
    gout = gout.reshape(-1, depth)
    pre = jnp.transpose(preact, (1, 2, 0, 3))
    act = jnp.transpose(activation, (1, 2, 0, 3))
    fine_of = jnp.arange(2 * depth)[None, :] // 2 == jnp.arange(depth)[:, None]
    up = jnp.where(fine_of, 0.125, 0.0).astype(BF)
    down = fine_of.T.astype(BF)
    vmem = pl.BlockSpec(memory_space=pltpu.VMEM)
    dma = pltpu.SemaphoreType.DMA
    out, gwa, gwb = pl.pallas_call(
        kernel,
        out_shape=(
            jax.ShapeDtypeStruct((2, 16, 32, 256), BF),
            jax.ShapeDtypeStruct((NXY, 16, 128), F32),
            jax.ShapeDtypeStruct((2, 48, 128), F32),
        ),
        in_specs=[vmem] * 7,
        out_specs=(vmem,) * 3,
        scratch_shapes=[
            pltpu.VMEM((NF, 4, 80, 128), BF),
            pltpu.VMEM((NF, 96, 128), BF),
            pltpu.VMEM((192, 1024), BF),
            pltpu.VMEM((384, 512), BF),
            pltpu.VMEM((4, 18, 32, 256), BF),
            pltpu.VMEM((3, 10, 32, 128), BF),
            pltpu.VMEM((4, 18, 32, 256), BF),
            pltpu.VMEM((8, 512, 256), BF),
            pltpu.VMEM((512, 512), F32),
            pltpu.VMEM((NXY, 48, 128), BF),
            pltpu.VMEM((NXY, 48, 128), BF),
            pltpu.VMEM((NXY, 48, 128), BF),
            pltpu.VMEM((48, 128), BF),
            pltpu.VMEM((2, 48, 128), F32),
            pltpu.VMEM((NXY, 16, 128), BF),
            pltpu.VMEM((NXY, 16, 128), BF),
            pltpu.VMEM((NXY, 16, 128), BF),
            pltpu.VMEM((NXY, 16, 128), BF),
            pltpu.VMEM((16, 128), BF),
            dma((3, NF)),
            dma((3, NF)),
            dma((NF,)),
            dma((NF,)),
            dma((8,)),
            dma((8,)),
            dma((8,)),
            dma((8,)),
            dma((NXY,)),
            dma((NXY,)),
            dma((2,)),
            dma((NXY,)),
            dma((NXY,)),
            dma((2,)),
            dma((NXY,)),
            dma((NXY,)),
            dma((NXY,)),
            dma((NXY,)),
            dma((NXY,)),
            dma((NXY,)),
        ],
        compiler_params=pltpu.CompilerParams(
            collective_id=0, has_side_effects=True, vmem_limit_bytes=48 * 1024 * 1024
        ),
    )(gout, pre, act, tap_rows(weight_a), tap_rows(weight_b), up, down)
    grad_input = jnp.transpose(out, (2, 0, 1, 3))
    packed = gwa.reshape(256, 128)
    rest = packed[:216, 96:].reshape(3, 72, 32).transpose(1, 0, 2).reshape(72, 96)
    full = jnp.concatenate([packed[:216, :96], rest], axis=0)
    full = full.reshape(3, 3, 32, 3, 32)[::-1, ::-1]
    grad_wa = jnp.transpose(full, (0, 1, 3, 2, 4)).reshape(27, 32, 32)
    part = gwb.reshape(96, 128)[:72, :96].reshape(3, 3, 8, 3, 32)[::-1, ::-1]
    grad_wb = jnp.transpose(part, (0, 1, 3, 2, 4)).reshape(27, 8, 32)
    return (grad_input, grad_wa, grad_wb)


def solution(mesh):
    placed = (
        P(None, "space", "filt", None),
        P(None, "space", "filt", None),
        P("filt", "space", None, None),
        P(),
        P(None, "filt", None),
    )
    return jax.shard_map(
        per_device,
        mesh=mesh,
        in_specs=placed,
        out_specs=(P(None, "space", "filt", None), P(), P(None, "filt", None)),
        check_vma=False,
    )
```

```python
import math

import jax
import jax.numpy as jnp
from jax import lax
from jax.experimental import pallas as pl
from jax.experimental.pallas import tpu as pltpu
from jax.sharding import PartitionSpec as P

BF = jnp.bfloat16
F32 = jnp.float32
NF = 8
ROWS = 8
NXY = 16
PRE_AT = 5


def shifted(values, step):
    width = values.shape[-1]
    axis = values.ndim - 1
    lane = lax.broadcasted_iota(jnp.int32, values.shape, axis)
    rolled = pltpu.roll(values, step % width, axis)
    edge = 0 if step == 1 else width - 1
    return jnp.where(lane == edge, 0.0, rolled)


def kernel(
    gout_h,
    pre_h,
    act_h,
    wa_h,
    wb_h,
    out_t,
    gwa_out,
    gwb_out,
    graw,
    praw,
    araw,
    waraw,
    wbraw,
    gsrc,
    wb0,
    grid_b,
    wb_all,
    tb,
    ta,
    prh,
    pool,
    pool2,
    pcat,
    gpo,
    gpc,
    gp,
    actt,
    act3,
    racc,
    out_v,
    gwb,
    rb1,
    rb2,
    sb,
    fin,
    gwa,
    ra1,
    ra2,
    ra3,
    sa,
    sin,
    s1,
    r1,
    sf,
    rf,
    sw,
    rw,
    sx,
    spool,
    rpool,
    sp,
    rp,
    sc,
    rc,
    sb1,
    qb1,
    sb2,
    qb2,
    sb3,
    qb3,
    sa1,
    qa1,
    sa2,
    qa2,
    sa3,
    qa3,
):
    f = lax.axis_index("filt")
    p = lax.axis_index("space")
    ns = lax.axis_size("space")
    xy = p // 2
    zl = p % 2
    me2 = f * 2 + zl

    def fmod(v):
        return lax.rem(v + NF, NF)

    def smod(v):
        return lax.rem(v + ns, ns)

    def xymod(v):
        return lax.rem(v + NXY, NXY)

    def send(src, dst, ss, rs, tf, tp):
        pltpu.make_async_remote_copy(
            src_ref=src,
            dst_ref=dst,
            send_sem=ss,
            recv_sem=rs,
            device_id={"filt": tf, "space": tp},
            device_id_type=pl.DeviceIdType.MESH,
        ).start()

    def wait(ref, sem):
        pltpu.make_async_copy(ref, ref, sem).wait()

    barrier = pltpu.get_barrier_semaphore()

    def greet(tf, tp):
        pl.semaphore_signal(
            barrier,
            inc=1,
            device_id={"filt": tf, "space": tp},
            device_id_type=pl.DeviceIdType.MESH,
        )

    @pl.loop(1, NXY)
    def _(j):
        t = xymod(me2 + j)
        greet(t // 2, xy * 2 + lax.rem(t, 2))

    @pl.loop(1, NXY)
    def _(j):
        greet(f, xymod(xy + j) * 2 + zl)

    cross = xymod(xy + 2 * zl - 1) * 2 + 1 - zl
    greet(f, cross)
    greet(fmod(f - 1), cross)
    greet(fmod(f + 1), cross)
    greet(fmod(f - 1), xymod(xy + 1) * 2 + zl)
    greet(fmod(f + 1), xymod(xy - 1) * 2 + zl)

    loads = [
        pltpu.make_async_copy(src, dst, sin.at[n])
        for n, (src, dst) in enumerate(
            ((gout_h, graw), (wb_h, wbraw), (pre_h, praw), (wa_h, waraw), (act_h, araw))
        )
    ]
    for load in loads:
        load.start()

    def selection(rows, per, high, low):
        row = lax.broadcasted_iota(jnp.int32, (rows, 4 * high), 0)
        col = lax.broadcasted_iota(jnp.int32, (rows, 4 * high), 1)
        tap = lax.shift_right_logical(row, per.bit_length() - 1)
        dx = lax.shift_right_logical(tap * 11, 5)
        dy = tap - 3 * dx
        place = (2 - dx) * high + (2 - dy) * low + (row - tap * per)
        return jnp.where(col == place, 1.0, 0.0).astype(BF)

    def arranged(raw, per, high, low):
        place = selection(9 * per, per, high, low)
        parts = []
        for dz in range(3):
            tall = jnp.concatenate([raw[3 * k + dz].astype(F32) for k in range(9)], axis=0)
            parts.append(
                lax.dot_general(
                    tall.astype(BF),
                    place,
                    (((0,), (0,)), ((), ())),
                    preferred_element_type=F32,
                )
            )
        return jnp.concatenate(parts, axis=0)

    loads[0].wait()
    rows = jnp.swapaxes(graw[...].astype(F32), 0, 1).reshape(512, 128)
    edge = jnp.zeros((8, 128), F32)
    gsrc[...] = jnp.concatenate([edge, rows, edge], axis=0).astype(BF)
    loads[1].wait()
    wb0[...] = arranged(wbraw, 8, 32, 8).astype(BF)

    pl.semaphore_wait(barrier, 2 * (NXY - 1) + 5)

    core = lax.rem(f, 2)
    sibling = f + 1 - 2 * core

    @pl.loop(1, 4)
    def _(j):
        send(wb0, wb_all.at[f], sw.at[j], rw.at[f], fmod(f + 2 * j), p)

    send(wb0, wb_all.at[f], sx.at[0], rw.at[f], sibling, p)
    wb_all[f] = wb0[...]

    def block(t):
        return gsrc.at[pl.ds(pl.multiple_of(t * 32, 16), 48)]

    @pl.loop(1, NXY)
    def _(j):
        t = xymod(me2 + j)
        send(
            block(t),
            grid_b.at[f, 1 + zl],
            s1.at[j],
            r1.at[me2],
            t // 2,
            xy * 2 + lax.rem(t, 2),
        )

    loads[2].wait()
    for x in range(2):
        turned = jnp.swapaxes(praw[:, x].astype(F32), 0, 1)
        prh[1 + x, 1:17] = turned.astype(BF)

    pre_moves = (
        (prh.at[1, pl.ds(1, 16)], prh.at[3, pl.ds(1, 16)], 0, -1),
        (prh.at[2, pl.ds(1, 16)], prh.at[0, pl.ds(1, 16)], 0, 1),
        (prh.at[pl.ds(1, 2), 1], prh.at[pl.ds(1, 2), 17], -1, 0),
        (prh.at[pl.ds(1, 2), 16], prh.at[pl.ds(1, 2), 0], 1, 0),
        (prh.at[1, 1], prh.at[3, 17], -1, -1),
        (prh.at[1, 16], prh.at[3, 0], 1, -1),
        (prh.at[2, 1], prh.at[0, 17], -1, 1),
        (prh.at[2, 16], prh.at[0, 0], 1, 1),
    )

    def send_pre(first=0, last=8):
        for n in range(first, last):
            src, dst, df, dp = pre_moves[n]
            send(src, dst, sp.at[n], rp.at[n], fmod(f + df), smod(p + dp))

    if PRE_AT == 0:
        send_pre()

    grid_b[f, 1 + zl] = gsrc[pl.ds(pl.multiple_of(me2 * 32, 16), 48)]

    def forward(s):
        sz = lax.rem(s, 2)
        send(
            grid_b.at[s // 2, 1 + sz],
            grid_b.at[s // 2, 3 - 3 * sz],
            sf.at[s],
            rf.at[s],
            f,
            xymod(xy + 2 * sz - 1) * 2 + zl,
        )

    forward(me2)

    fine_row = lax.broadcasted_iota(jnp.int32, (256, 128), 0)
    fine_col = lax.broadcasted_iota(jnp.int32, (256, 128), 1)
    down = jnp.where(lax.shift_right_logical(fine_row, 1) == fine_col, 1.0, 0.0).astype(BF)
    total = jnp.zeros((ROWS * 32, 128), F32)
    for x2 in range(2):
        relu = jnp.maximum(prh[1 + x2, 1:17], jnp.zeros((), BF)).reshape(ROWS, 2, 32, 256)
        for y2 in range(2):
            total += jnp.dot(
                relu[:, y2].reshape(ROWS * 32, 256), down, preferred_element_type=F32
            )
    pool[...] = (total * 0.125).astype(BF).reshape(ROWS, 32, 128)
    send(
        pool.at[pl.ds(4 - 4 * zl, 4)],
        pool2.at[zl],
        spool.at[0],
        rpool.at[0],
        f,
        xy * 2 + 1 - zl,
    )
    pool2[zl] = pool[pl.ds(4 * zl, 4)]

    if PRE_AT == 7:
        send_pre(0, 1)
    @pl.loop(1, 4)
    def _(j):
        s = fmod(f - 2 * j)
        wait(wb0, rw.at[s])
        send(wb_all.at[s], wb_all.at[s], sx.at[j], rw.at[s], sibling, p)

    if PRE_AT == 5:
        send_pre()
    if PRE_AT == 6:
        send_pre(0, 1)
    @pl.loop(1, NXY)
    def _(j):
        s = xymod(me2 - j)
        wait(grid_b.at[0, 0], r1.at[s])
        forward(s)

    if PRE_AT == 1:
        send_pre()
    if PRE_AT in (6, 7):
        send_pre(1, 8)

    loads[3].wait()
    wide_a = arranged(waraw, 32, 128, 32)
    for n, turn in enumerate((0, 32, 128, 160)):
        ta[n * 96 : n * 96 + 96] = (
            pltpu.roll(wide_a, turn, 1) if turn else wide_a
        ).astype(BF)

    @pl.loop(0, 4)
    def _(j):
        wait(wb0, rw.at[2 * j + 1 - core])

    for n in range(NF):
        wide_b = wb_all[n].astype(F32)
        for k, turn in enumerate((0, 8, 32, 40)):
            tb[k * 96 : k * 96 + 96, n * 128 : n * 128 + 128] = (
                pltpu.roll(wide_b, turn, 1) if turn else wide_b
            ).astype(BF)

    @pl.loop(0, NXY)
    def _(j):
        wait(grid_b.at[0, 0], rf.at[j])

    @pl.when(xy == 0)
    def _():
        grid_b[:, 0] = jnp.zeros((NF,) + grid_b.shape[2:], BF)

    @pl.when(xy == NXY - 1)
    def _():
        grid_b[:, 3] = jnp.zeros((NF,) + grid_b.shape[2:], BF)

    g_cat = jnp.concatenate(
        [grid_b[:, :, 16 * b : 16 * b + 32, :].reshape(1024, 128) for b in range(2)], axis=1
    )
    prod = jnp.dot(tb[...], g_cat, preferred_element_type=F32)
    for b in range(2):
        term = prod[:, b * 128 : b * 128 + 128].reshape(2, 2, 3, 32, 128)
        rows = term[:, :, 1] + shifted(term[:, :, 0], -1) + shifted(term[:, :, 2], 1)
        gpo[:, 2 * b : 2 * b + 2] = rows.astype(BF)

    right = xymod(xy + 1) * 2
    left = xymod(xy - 1) * 2 + 1
    step = fmod(f + 2 * zl - 1)
    own_rows = pl.ds(1 + 4 * zl, 4)
    far = 9 - 9 * zl
    both = pl.ds(0, 2)
    coarse_moves = (
        (gpo, gpc.at[pl.ds(zl, 2), own_rows], 0, f, xy * 2 + 1 - zl),
        (gpo.at[1], gpc.at[0, own_rows], 1 + zl, f, right),
        (gpo.at[0], gpc.at[2, own_rows], 1 + zl, f, left),
        (gpo.at[both, 3 * zl], gpc.at[pl.ds(1, 2), far], 3 + zl, step, xy * 2),
        (gpo.at[both, 3 * zl], gpc.at[pl.ds(0, 2), far], 3 + zl, step, xy * 2 + 1),
        (gpo.at[1, 3 * zl], gpc.at[0, far], 5 + zl, step, right),
        (gpo.at[0, 3 * zl], gpc.at[2, far], 5 + zl, step, left),
    )
    for n, (src, dst, slot, tf, tp) in enumerate(coarse_moves):
        send(src, dst, sc.at[n], rc.at[slot], tf, tp)
    gpc[pl.ds(1 - zl, 2), own_rows] = gpo[...]

    wait(pool2.at[0], rpool.at[0])
    mid = pool2[...].reshape(256, 128).astype(F32)
    for k, version in enumerate((shifted(mid, 1), mid, shifted(mid, -1), jnp.zeros_like(mid))):
        version = version.astype(BF).reshape(2, 2, 2, 32, 128)
        for x2 in range(2):
            for b in range(2):
                for y2 in range(2):
                    r0 = (x2 * 2 + y2) * 128 + k * 32
                    pcat[r0 : r0 + 32, b * 128 : b * 128 + 128] = version[x2, b, y2]
    pairs = lax.dot_general(
        g_cat, pcat[...], (((1,), (1,)), ((), ())), preferred_element_type=F32
    ).reshape(NF, 4, 4, 8, 512)
    folded = None
    for x2 in range(2):
        for y2 in range(2):
            c0 = (x2 * 2 + y2) * 128
            term = pairs[:, x2 : x2 + 3, y2 : y2 + 3, :, c0 : c0 + 128]
            folded = term if folded is None else folded + term
    folded = jnp.concatenate(
        [folded.reshape(NF, 72, 128), jnp.zeros((NF, 24, 128), F32)], axis=1
    )
    gwb[...] = folded.astype(BF).reshape(2 * NF, 48, 128)

    @pl.loop(1, NXY)
    def _(j):
        k = xymod(xy + j)
        send(gwb.at[k], rb1.at[xy], sb1.at[j], qb1.at[xy], f, k * 2 + zl)

    rb1[xy] = gwb[xy]

    loads[4].wait()
    for x in range(2):
        actt[x] = jnp.swapaxes(araw[:, x].astype(F32), 0, 1)

    @pl.loop(0, 8)
    def _(b):
        for x2 in range(2):
            for y2 in range(2):
                wide = actt[x2, 2 * b + y2]
                base = (x2 * 2 + y2) * 128
                act3[b, base : base + 32] = shifted(wide, 1).astype(BF)
                act3[b, base + 32 : base + 64] = wide.astype(BF)
                act3[b, base + 64 : base + 96] = shifted(wide, -1).astype(BF)
                act3[b, base + 96 : base + 128] = jnp.zeros((32, 256), BF)

    @pl.loop(1, NXY)
    def _(j):
        wait(rb1.at[0], qb1.at[xymod(xy + j)])

    owner = xy // 2
    sb[...] = jnp.sum(rb1[...].astype(F32), axis=0).astype(BF)
    for zt in range(2):

        @pl.when((f != owner) | (zl != zt))
        def _():
            send(sb, rb2.at[me2], sb2.at[zt], qb2.at[me2], owner, xy * 2 + zt)

    wait(gpo, rc.at[0])
    for n in range(2):
        wait(gpo.at[0], rc.at[1 + n])
        wait(gpo.at[both, 0], rc.at[3 + n])
        wait(gpo.at[0, 0], rc.at[5 + n])
    for n, (src, dst, df, dp) in enumerate(pre_moves):
        wait(dst, rp.at[n])

    @pl.when(p == 0)
    def _():
        prh[0] = jnp.zeros(prh.shape[1:], BF)

    @pl.when(p == ns - 1)
    def _():
        prh[3] = jnp.zeros(prh.shape[1:], BF)

    @pl.when(f == 0)
    def _():
        prh[:, 0] = jnp.zeros((4, 32, 256), BF)

    @pl.when(f == NF - 1)
    def _():
        prh[:, 17] = jnp.zeros((4, 32, 256), BF)

    up_row = lax.broadcasted_iota(jnp.int32, (128, 256), 0)
    up_col = lax.broadcasted_iota(jnp.int32, (128, 256), 1)
    up = jnp.where(lax.shift_right_logical(up_col, 1) == up_row, 0.125, 0.0).astype(BF)
    for plane in range(3):
        fine = (
            jnp.dot(gpc[plane].reshape(320, 128), up, preferred_element_type=F32)
            .astype(BF)
            .reshape(10, 32, 256)
        )
        for xh in ((0,), (1, 2), (3,))[plane]:
            for row in range(10):
                for yh in (2 * row - 1, 2 * row):
                    if 0 <= yh <= 17:
                        gp[xh, yh] = jnp.where(
                            prh[xh, yh] > jnp.zeros((), BF), fine[row], jnp.zeros((), BF)
                        )

    racc[...] = jnp.zeros(racc.shape, F32)

    @pl.loop(0, 8)
    def _(b):
        cells = gp[:, pl.ds(2 * b, 4)].reshape(512, 256)
        racc[...] += lax.dot_general(
            cells, act3[b], (((1,), (1,)), ((), ())), preferred_element_type=F32
        )

    taps = []
    for dx in range(3):
        for dy in range(3):
            term = None
            for x2 in range(2):
                for y2 in range(2):
                    r0 = ((x2 + dx) * 4 + y2 + dy) * 32
                    c0 = (x2 * 2 + y2) * 128
                    piece = racc[r0 : r0 + 32, c0 : c0 + 128]
                    term = piece if term is None else term + piece
            taps.append(term)
    full = jnp.concatenate(taps, axis=0)
    rest = full[216:288]
    tail = jnp.concatenate([pltpu.roll(rest, turn, 1) for turn in (96, 64, 32)], axis=0)
    lane = lax.broadcasted_iota(jnp.int32, (216, 128), 1)
    packed = jnp.where(lane < 96, full[:216], tail)
    packed = jnp.concatenate([packed, jnp.zeros((40, 128), F32)], axis=0)
    gwa[...] = packed.astype(BF).reshape(NXY, 16, 128)

    @pl.loop(1, NXY)
    def _(j):
        k = xymod(xy + j)
        send(gwa.at[k], ra1.at[xy], sa1.at[j], qa1.at[xy], f, k * 2 + zl)

    ra1[xy] = gwa[xy]

    half = lax.rem(xy, 2)

    @pl.when(f == owner)
    def _():
        rb2[me2] = sb[...]

        @pl.loop(1, NXY)
        def _(j):
            wait(rb2.at[0], qb2.at[xymod(me2 + j)])

        fin[half] = jnp.sum(rb2[...].astype(F32), axis=0)

        @pl.loop(1, NXY)
        def _(j):
            send(fin.at[half], fin.at[half], sb3.at[j], qb3.at[half], f, xymod(xy + j) * 2 + zl)

    @pl.loop(0, 8)
    def _(b):
        cells = gp[:, pl.ds(2 * b, 4)].reshape(512, 256)
        term = jnp.dot(ta[...], cells, preferred_element_type=F32).reshape(2, 2, 3, 32, 256)
        rows = term[:, :, 1] + shifted(term[:, :, 0], -1) + shifted(term[:, :, 2], 1)
        out_v[:, pl.ds(2 * b, 2)] = rows.astype(BF)

    for x in range(2):
        turned = jnp.swapaxes(out_v[x].astype(F32), 0, 1)
        out_t[:, x] = turned.astype(BF)


    @pl.loop(1, NXY)
    def _(j):
        wait(ra1.at[0], qa1.at[xymod(xy + j)])

    sa[...] = jnp.sum(ra1[...].astype(F32), axis=0).astype(BF)

    @pl.loop(1, NXY)
    def _(j):
        t = xymod(me2 + j)
        send(sa, ra2.at[me2], sa2.at[j], qa2.at[me2], t // 2, xy * 2 + lax.rem(t, 2))

    ra2[me2] = sa[...]

    @pl.loop(1, NXY)
    def _(j):
        wait(ra2.at[0], qa2.at[xymod(me2 + j)])

    ra3[xy] = jnp.sum(ra2[...].astype(F32), axis=0).astype(BF)

    @pl.loop(1, NXY)
    def _(j):
        k = xymod(xy + j)
        send(ra3.at[xy], ra3.at[xy], sa3.at[j], qa3.at[xy], f, k * 2 + zl)

    for h in range(2):

        @pl.when(xy != 2 * f + h)
        def _():
            wait(fin.at[h], qb3.at[h])

    scale_b = 1.0 / math.sqrt(ns * NF * ROWS * 128)
    scale_a = 1.0 / math.sqrt(8 * ns * NF * ROWS * 128)

    def unfold(full, per, target, scale):
        for dx in range(3):
            for dy in range(3):
                r0 = ((2 - dx) * 3 + 2 - dy) * per
                for dz in range(3):
                    target[9 * dx + 3 * dy + dz] = (
                        full[r0 : r0 + per, dz * 32 : dz * 32 + 32] * scale
                    )

    unfold(fin[...].reshape(96, 128), 8, gwb_out, scale_b)

    @pl.loop(1, NXY)
    def _(j):
        wait(grid_b.at[0, 0], s1.at[j])
        wait(gwb.at[0], sb1.at[j])
        wait(gwa.at[0], sa1.at[j])
        wait(sa, sa2.at[j])

    @pl.loop(0, NXY)
    def _(j):
        wait(grid_b.at[0, 0], sf.at[j])

    @pl.loop(1, 4)
    def _(j):
        wait(wb0, sw.at[j])

    @pl.loop(0, 4)
    def _(j):
        wait(wb0, sx.at[j])

    wait(pool2.at[0], spool.at[0])
    for n, (src, dst, df, dp) in enumerate(pre_moves):
        wait(src, sp.at[n])
    for n, (src, dst, slot, tf, tp) in enumerate(coarse_moves):
        wait(src, sc.at[n])

    for zt in range(2):

        @pl.when((f != owner) | (zl != zt))
        def _():
            wait(sb, sb2.at[zt])

    @pl.when(f == owner)
    def _():
        @pl.loop(1, NXY)
        def _(j):
            wait(fin.at[0], sb3.at[j])


    @pl.loop(1, NXY)
    def _(j):
        wait(ra3.at[0], qa3.at[xymod(xy + j)])

    packed = ra3[...].astype(F32).reshape(256, 128)
    rest = None
    lane = lax.broadcasted_iota(jnp.int32, (72, 128), 1)
    for n in range(3):
        piece = pltpu.roll(packed[n * 72 : n * 72 + 72], 32 * (n + 1), 1)
        rest = piece if n == 0 else jnp.where(lane < 32 * n, rest, piece)
    full = jnp.concatenate([packed[:216], rest], axis=0)
    unfold(full, 32, gwa_out, scale_a)

    @pl.loop(1, NXY)
    def _(j):
        wait(ra3.at[0], sa3.at[j])


def per_device(activation, preact, grad_out, weight_a, weight_b):
    hbm = pl.BlockSpec(memory_space=pltpu.HBM)
    vmem = pl.BlockSpec(memory_space=pltpu.VMEM)
    dma = pltpu.SemaphoreType.DMA
    out, gwa, gwb = pl.pallas_call(
        kernel,
        out_shape=(
            jax.ShapeDtypeStruct((32, 2, 16, 256), BF),
            jax.ShapeDtypeStruct((27, 32, 32), F32),
            jax.ShapeDtypeStruct((27, 8, 32), F32),
        ),
        in_specs=[hbm] * 5,
        out_specs=(vmem,) * 3,
        scratch_shapes=[
            pltpu.VMEM((8, 64, 128), BF),
            pltpu.VMEM((32, 2, 16, 256), BF),
            pltpu.VMEM((32, 2, 16, 256), BF),
            pltpu.VMEM((27, 32, 32), BF),
            pltpu.VMEM((27, 8, 32), BF),
            pltpu.VMEM((528, 128), BF),
            pltpu.VMEM((96, 128), BF),
            pltpu.VMEM((NF, 4, 48, 128), BF),
            pltpu.VMEM((NF, 96, 128), BF),
            pltpu.VMEM((384, 1024), BF),
            pltpu.VMEM((384, 512), BF),
            pltpu.VMEM((4, 18, 32, 256), BF),
            pltpu.VMEM((ROWS, 32, 128), BF),
            pltpu.VMEM((2, 4, 32, 128), BF),
            pltpu.VMEM((512, 256), BF),
            pltpu.VMEM((2, 4, 32, 128), BF),
            pltpu.VMEM((3, 10, 32, 128), BF),
            pltpu.VMEM((4, 18, 32, 256), BF),
            pltpu.VMEM((2, 16, 32, 256), F32),
            pltpu.VMEM((8, 512, 256), BF),
            pltpu.VMEM((512, 512), F32),
            pltpu.VMEM((2, 16, 32, 256), BF),
            pltpu.VMEM((NXY, 48, 128), BF),
            pltpu.VMEM((NXY, 48, 128), BF),
            pltpu.VMEM((NXY, 48, 128), BF),
            pltpu.VMEM((48, 128), BF),
            pltpu.VMEM((2, 48, 128), F32),
            pltpu.VMEM((NXY, 16, 128), BF),
            pltpu.VMEM((NXY, 16, 128), BF),
            pltpu.VMEM((NXY, 16, 128), BF),
            pltpu.VMEM((NXY, 16, 128), BF),
            pltpu.VMEM((16, 128), BF),
            dma((5,)),
            dma((NXY,)),
            dma((NXY,)),
            dma((NXY,)),
            dma((NXY,)),
            dma((NF,)),
            dma((NF,)),
            dma((4,)),
            dma((1,)),
            dma((1,)),
            dma((8,)),
            dma((8,)),
            dma((7,)),
            dma((7,)),
            dma((NXY,)),
            dma((NXY,)),
            dma((2,)),
            dma((NXY,)),
            dma((NXY,)),
            dma((2,)),
            dma((NXY,)),
            dma((NXY,)),
            dma((NXY,)),
            dma((NXY,)),
            dma((NXY,)),
            dma((NXY,)),
        ],
        compiler_params=pltpu.CompilerParams(
            collective_id=0, has_side_effects=True, vmem_limit_bytes=32 * 1024 * 1024
        ),
    )(
        *(
            pltpu.with_memory_space_constraint(x, pltpu.HBM)
            for x in (grad_out.reshape(8, 64, 128), preact, activation, weight_a, weight_b)
        )
    )
    return (out, gwa, gwb)


def solution(mesh):
    placed = (
        P(None, "space", "filt", None),
        P(None, "space", "filt", None),
        P("filt", "space", None, None),
        P(),
        P(None, "filt", None),
    )
    return jax.shard_map(
        per_device,
        mesh=mesh,
        in_specs=placed,
        out_specs=(P(None, "space", "filt", None), P(), P(None, "filt", None)),
        check_vma=False,
    )
```

```python
import math

import jax
import jax.numpy as jnp
from jax import lax
from jax.experimental import pallas as pl
from jax.experimental.pallas import tpu as pltpu
from jax.sharding import PartitionSpec as P

BF = jnp.bfloat16
F32 = jnp.float32
NF = 8
ROWS = 8
NXY = 16


FAR_XY = (10, 9, 11, 6, 14, 8, 2, 5, 7, 13, 15, 1, 3, 4, 12)
FAR_Z = (8, 7, 9, 6, 10, 5, 11, 4, 12, 3, 13, 14, 15, 1, 2)


def shifted(values, step):
    width = values.shape[-1]
    axis = values.ndim - 1
    lane = lax.broadcasted_iota(jnp.int32, values.shape, axis)
    rolled = pltpu.roll(values, step % width, axis)
    edge = 0 if step == 1 else width - 1
    return jnp.where(lane == edge, 0.0, rolled)


def kernel(
    gout_h,
    pre_h,
    act_h,
    wa_h,
    wb_h,
    out_t,
    gwa_out,
    gwb_out,
    graw,
    praw,
    araw,
    waraw,
    wbraw,
    gsrc,
    wb0,
    grid_b,
    wb_all,
    tb,
    ta,
    prh,
    pool,
    pool2,
    pcat,
    gpo,
    gpc,
    gp,
    actt,
    act3,
    racc,
    out_v,
    gwb,
    rb1,
    rb2,
    sb,
    fin,
    gwa,
    ra1,
    ra2,
    ra3,
    sa,
    sin,
    s1,
    r1,
    sf,
    rf,
    sw,
    rw,
    sx,
    spool,
    rpool,
    sp,
    rp,
    sc,
    rc,
    sb1,
    qb1,
    sb2,
    qb2,
    sb3,
    qb3,
    sa1,
    qa1,
    sa2,
    qa2,
    sa3,
    qa3,
):
    f = lax.axis_index("filt")
    p = lax.axis_index("space")
    ns = lax.axis_size("space")
    xy = p // 2
    zl = p % 2
    me2 = f * 2 + zl

    def fmod(v):
        return lax.rem(v + NF, NF)

    def smod(v):
        return lax.rem(v + ns, ns)

    def xymod(v):
        return lax.rem(v + NXY, NXY)

    def send(src, dst, ss, rs, tf, tp):
        pltpu.make_async_remote_copy(
            src_ref=src,
            dst_ref=dst,
            send_sem=ss,
            recv_sem=rs,
            device_id={"filt": tf, "space": tp},
            device_id_type=pl.DeviceIdType.MESH,
        ).start()

    def wait(ref, sem):
        pltpu.make_async_copy(ref, ref, sem).wait()

    barrier = pltpu.get_barrier_semaphore()

    def greet(tf, tp):
        pl.semaphore_signal(
            barrier,
            inc=1,
            device_id={"filt": tf, "space": tp},
            device_id_type=pl.DeviceIdType.MESH,
        )

    cross = xymod(xy + 2 * zl - 1) * 2 + 1 - zl
    greet(f, cross)
    greet(fmod(f - 1), cross)
    greet(fmod(f + 1), cross)
    greet(fmod(f - 1), xymod(xy + 1) * 2 + zl)
    greet(fmod(f + 1), xymod(xy - 1) * 2 + zl)

    @pl.loop(1, NXY)
    def _(j):
        t = xymod(me2 + j)
        greet(t // 2, xy * 2 + lax.rem(t, 2))

    @pl.loop(1, NXY)
    def _(j):
        greet(f, xymod(xy + j) * 2 + zl)

    loads = [
        pltpu.make_async_copy(src, dst, sin.at[n])
        for n, (src, dst) in enumerate(
            ((gout_h, graw), (wb_h, wbraw), (pre_h, praw), (wa_h, waraw), (act_h, araw))
        )
    ]
    for load in loads:
        load.start()

    def selection(rows, per, high, low):
        row = lax.broadcasted_iota(jnp.int32, (rows, 4 * high), 0)
        col = lax.broadcasted_iota(jnp.int32, (rows, 4 * high), 1)
        tap = lax.shift_right_logical(row, per.bit_length() - 1)
        dx = lax.shift_right_logical(tap * 11, 5)
        dy = tap - 3 * dx
        place = (2 - dx) * high + (2 - dy) * low + (row - tap * per)
        return jnp.where(col == place, 1.0, 0.0).astype(BF)

    def arranged(raw, per, high, low):
        place = selection(9 * per, per, high, low)
        parts = []
        for dz in range(3):
            tall = jnp.concatenate([raw[3 * k + dz].astype(F32) for k in range(9)], axis=0)
            parts.append(
                lax.dot_general(
                    tall.astype(BF),
                    place,
                    (((0,), (0,)), ((), ())),
                    preferred_element_type=F32,
                )
            )
        return jnp.concatenate(parts, axis=0)

    loads[0].wait()
    rows = jnp.swapaxes(graw[...].astype(F32), 0, 1).reshape(512, 128)
    edge = jnp.zeros((8, 128), F32)
    gsrc[...] = jnp.concatenate([edge, rows, edge], axis=0).astype(BF)
    loads[1].wait()
    wb0[...] = arranged(wbraw, 8, 32, 8).astype(BF)

    pl.semaphore_wait(barrier, 2 * (NXY - 1) + 5)

    core = lax.rem(f, 2)
    sibling = f + 1 - 2 * core

    @pl.loop(1, 4)
    def _(j):
        send(wb0, wb_all.at[f], sw.at[j], rw.at[f], fmod(f + 2 * j), p)

    send(wb0, wb_all.at[f], sx.at[0], rw.at[f], sibling, p)
    wb_all[f] = wb0[...]

    def block(t):
        return gsrc.at[pl.ds(pl.multiple_of(t * 32, 16), 48)]

    @pl.loop(1, NXY)
    def _(j):
        t = xymod(me2 + j)
        send(
            block(t),
            grid_b.at[f, 1 + zl],
            s1.at[j],
            r1.at[me2],
            t // 2,
            xy * 2 + lax.rem(t, 2),
        )

    loads[2].wait()
    for x in range(2):
        turned = jnp.swapaxes(praw[:, x].astype(F32), 0, 1)
        prh[1 + x, 1:17] = turned.astype(BF)

    pre_moves = (
        (prh.at[1, pl.ds(1, 16)], prh.at[3, pl.ds(1, 16)], 0, -1),
        (prh.at[2, pl.ds(1, 16)], prh.at[0, pl.ds(1, 16)], 0, 1),
        (prh.at[pl.ds(1, 2), 1], prh.at[pl.ds(1, 2), 17], -1, 0),
        (prh.at[pl.ds(1, 2), 16], prh.at[pl.ds(1, 2), 0], 1, 0),
        (prh.at[1, 1], prh.at[3, 17], -1, -1),
        (prh.at[1, 16], prh.at[3, 0], 1, -1),
        (prh.at[2, 1], prh.at[0, 17], -1, 1),
        (prh.at[2, 16], prh.at[0, 0], 1, 1),
    )

    grid_b[f, 1 + zl] = gsrc[pl.ds(pl.multiple_of(me2 * 32, 16), 48)]

    def forward(s):
        sz = lax.rem(s, 2)
        send(
            grid_b.at[s // 2, 1 + sz],
            grid_b.at[s // 2, 3 - 3 * sz],
            sf.at[s],
            rf.at[s],
            f,
            xymod(xy + 2 * sz - 1) * 2 + zl,
        )

    forward(me2)

    fine_row = lax.broadcasted_iota(jnp.int32, (256, 128), 0)
    fine_col = lax.broadcasted_iota(jnp.int32, (256, 128), 1)
    down = jnp.where(lax.shift_right_logical(fine_row, 1) == fine_col, 1.0, 0.0).astype(BF)
    total = jnp.zeros((ROWS * 32, 128), F32)
    for x2 in range(2):
        relu = jnp.maximum(prh[1 + x2, 1:17], jnp.zeros((), BF)).reshape(ROWS, 2, 32, 256)
        for y2 in range(2):
            total += jnp.dot(
                relu[:, y2].reshape(ROWS * 32, 256), down, preferred_element_type=F32
            )
    pool[...] = (total * 0.125).astype(BF).reshape(ROWS, 32, 128)
    send(
        pool.at[pl.ds(4 - 4 * zl, 4)],
        pool2.at[zl],
        spool.at[0],
        rpool.at[0],
        f,
        xy * 2 + 1 - zl,
    )
    pool2[zl] = pool[pl.ds(4 * zl, 4)]

    @pl.loop(1, 4)
    def _(j):
        s = fmod(f - 2 * j)
        wait(wb0, rw.at[s])
        send(wb_all.at[s], wb_all.at[s], sx.at[j], rw.at[s], sibling, p)

    for n, (src, dst, df, dp) in enumerate(pre_moves):
        send(src, dst, sp.at[n], rp.at[n], fmod(f + df), smod(p + dp))

    @pl.loop(1, NXY)
    def _(j):
        s = xymod(me2 - j)
        wait(grid_b.at[0, 0], r1.at[s])
        forward(s)


    loads[3].wait()
    wide_a = arranged(waraw, 32, 128, 32)
    for n, turn in enumerate((0, 32, 128, 160)):
        ta[n * 96 : n * 96 + 96] = (
            pltpu.roll(wide_a, turn, 1) if turn else wide_a
        ).astype(BF)

    @pl.loop(0, 4)
    def _(j):
        wait(wb0, rw.at[2 * j + 1 - core])

    for n in range(NF):
        wide_b = wb_all[n].astype(F32)
        for k, turn in enumerate((0, 8, 32, 40)):
            tb[k * 96 : k * 96 + 96, n * 128 : n * 128 + 128] = (
                pltpu.roll(wide_b, turn, 1) if turn else wide_b
            ).astype(BF)

    @pl.loop(0, NXY)
    def _(j):
        wait(grid_b.at[0, 0], rf.at[j])

    @pl.when(xy == 0)
    def _():
        grid_b[:, 0] = jnp.zeros((NF,) + grid_b.shape[2:], BF)

    @pl.when(xy == NXY - 1)
    def _():
        grid_b[:, 3] = jnp.zeros((NF,) + grid_b.shape[2:], BF)

    g_cat = jnp.concatenate(
        [grid_b[:, :, 16 * b : 16 * b + 32, :].reshape(1024, 128) for b in range(2)], axis=1
    )
    prod = jnp.dot(tb[...], g_cat, preferred_element_type=F32)
    for b in range(2):
        term = prod[:, b * 128 : b * 128 + 128].reshape(2, 2, 3, 32, 128)
        rows = term[:, :, 1] + shifted(term[:, :, 0], -1) + shifted(term[:, :, 2], 1)
        gpo[:, 2 * b : 2 * b + 2] = rows.astype(BF)

    right = xymod(xy + 1) * 2
    left = xymod(xy - 1) * 2 + 1
    step = fmod(f + 2 * zl - 1)
    own_rows = pl.ds(1 + 4 * zl, 4)
    far = 9 - 9 * zl
    both = pl.ds(0, 2)
    coarse_moves = (
        (gpo, gpc.at[pl.ds(zl, 2), own_rows], 0, f, xy * 2 + 1 - zl),
        (gpo.at[1], gpc.at[0, own_rows], 1 + zl, f, right),
        (gpo.at[0], gpc.at[2, own_rows], 1 + zl, f, left),
        (gpo.at[both, 3 * zl], gpc.at[pl.ds(1, 2), far], 3 + zl, step, xy * 2),
        (gpo.at[both, 3 * zl], gpc.at[pl.ds(0, 2), far], 3 + zl, step, xy * 2 + 1),
        (gpo.at[1, 3 * zl], gpc.at[0, far], 5 + zl, step, right),
        (gpo.at[0, 3 * zl], gpc.at[2, far], 5 + zl, step, left),
    )
    for n, (src, dst, slot, tf, tp) in enumerate(coarse_moves):
        send(src, dst, sc.at[n], rc.at[slot], tf, tp)
    gpc[pl.ds(1 - zl, 2), own_rows] = gpo[...]

    wait(pool2.at[0], rpool.at[0])
    mid = pool2[...].reshape(256, 128).astype(F32)
    for k, version in enumerate((shifted(mid, 1), mid, shifted(mid, -1), jnp.zeros_like(mid))):
        version = version.astype(BF).reshape(2, 2, 2, 32, 128)
        for x2 in range(2):
            for b in range(2):
                for y2 in range(2):
                    r0 = (x2 * 2 + y2) * 128 + k * 32
                    pcat[r0 : r0 + 32, b * 128 : b * 128 + 128] = version[x2, b, y2]
    pairs = lax.dot_general(
        g_cat, pcat[...], (((1,), (1,)), ((), ())), preferred_element_type=F32
    ).reshape(NF, 4, 4, 8, 512)
    folded = None
    for x2 in range(2):
        for y2 in range(2):
            c0 = (x2 * 2 + y2) * 128
            term = pairs[:, x2 : x2 + 3, y2 : y2 + 3, :, c0 : c0 + 128]
            folded = term if folded is None else folded + term
    folded = jnp.concatenate(
        [folded.reshape(NF, 72, 128), jnp.zeros((NF, 24, 128), F32)], axis=1
    )
    gwb[...] = folded.astype(BF).reshape(2 * NF, 48, 128)

    @pl.loop(1, NXY)
    def _(j):
        k = xymod(xy + j)
        send(gwb.at[k], rb1.at[xy], sb1.at[j], qb1.at[xy], f, k * 2 + zl)

    rb1[xy] = gwb[xy]

    loads[4].wait()
    for x in range(2):
        actt[x] = jnp.swapaxes(araw[:, x].astype(F32), 0, 1)

    for b in range(8):
        for x2 in range(2):
            for y2 in range(2):
                wide = actt[x2, 2 * b + y2]
                r0, c0 = (x2 * 2 + y2) * 128, b * 256
                act3[r0 : r0 + 32, c0 : c0 + 256] = shifted(wide, 1).astype(BF)
                act3[r0 + 32 : r0 + 64, c0 : c0 + 256] = wide.astype(BF)
                act3[r0 + 64 : r0 + 96, c0 : c0 + 256] = shifted(wide, -1).astype(BF)
                act3[r0 + 96 : r0 + 128, c0 : c0 + 256] = jnp.zeros((32, 256), BF)

    @pl.loop(1, NXY)
    def _(j):
        wait(rb1.at[0], qb1.at[xymod(xy + j)])

    owner = xy // 2
    sb[...] = jnp.sum(rb1[...].astype(F32), axis=0).astype(BF)
    for zt in range(2):

        @pl.when((f != owner) | (zl != zt))
        def _():
            send(sb, rb2.at[me2], sb2.at[zt], qb2.at[me2], owner, xy * 2 + zt)

    wait(gpo, rc.at[0])
    for n in range(2):
        wait(gpo.at[0], rc.at[1 + n])
        wait(gpo.at[both, 0], rc.at[3 + n])
        wait(gpo.at[0, 0], rc.at[5 + n])
    for n, (src, dst, df, dp) in enumerate(pre_moves):
        wait(dst, rp.at[n])

    @pl.when(p == 0)
    def _():
        prh[0] = jnp.zeros(prh.shape[1:], BF)

    @pl.when(p == ns - 1)
    def _():
        prh[3] = jnp.zeros(prh.shape[1:], BF)

    @pl.when(f == 0)
    def _():
        prh[:, 0] = jnp.zeros((4, 32, 256), BF)

    @pl.when(f == NF - 1)
    def _():
        prh[:, 17] = jnp.zeros((4, 32, 256), BF)

    up_row = lax.broadcasted_iota(jnp.int32, (128, 256), 0)
    up_col = lax.broadcasted_iota(jnp.int32, (128, 256), 1)
    up = jnp.where(lax.shift_right_logical(up_col, 1) == up_row, 0.125, 0.0).astype(BF)
    for plane in range(3):
        fine = (
            jnp.dot(gpc[plane].reshape(320, 128), up, preferred_element_type=F32)
            .astype(BF)
            .reshape(10, 32, 256)
        )
        for xh in ((0,), (1, 2), (3,))[plane]:
            for row in range(10):
                for yh in (2 * row - 1, 2 * row):
                    if 0 <= yh <= 17:
                        gp[xh, yh] = jnp.where(
                            prh[xh, yh] > jnp.zeros((), BF), fine[row], jnp.zeros((), BF)
                        )

    cells = jnp.concatenate(
        [gp[:, 2 * b : 2 * b + 4].reshape(512, 256) for b in range(8)], axis=1
    )
    for x2 in range(2):
        r0, c0 = 128 * x2, 256 * x2
        racc[r0 : r0 + 384, c0 : c0 + 256] = lax.dot_general(
            cells[r0 : r0 + 384],
            act3[c0 : c0 + 256],
            (((1,), (1,)), ((), ())),
            preferred_element_type=F32,
        )

    taps = []
    for dx in range(3):
        for dy in range(3):
            term = None
            for x2 in range(2):
                for y2 in range(2):
                    r0 = ((x2 + dx) * 4 + y2 + dy) * 32
                    c0 = (x2 * 2 + y2) * 128
                    piece = racc[r0 : r0 + 32, c0 : c0 + 128]
                    term = piece if term is None else term + piece
            taps.append(term)
    full = jnp.concatenate(taps, axis=0)
    rest = full[216:288]
    tail = jnp.concatenate([pltpu.roll(rest, turn, 1) for turn in (96, 64, 32)], axis=0)
    lane = lax.broadcasted_iota(jnp.int32, (216, 128), 1)
    packed = jnp.where(lane < 96, full[:216], tail)
    packed = jnp.concatenate([packed, jnp.zeros((40, 128), F32)], axis=0)
    gwa[...] = packed.astype(BF).reshape(NXY, 16, 128)

    for j in FAR_XY:
        k = xymod(xy + j)
        send(gwa.at[k], ra1.at[xy], sa1.at[j], qa1.at[xy], f, k * 2 + zl)

    ra1[xy] = gwa[xy]

    half = lax.rem(xy, 2)

    @pl.when(f == owner)
    def _():
        rb2[me2] = sb[...]

        @pl.loop(1, NXY)
        def _(j):
            wait(rb2.at[0], qb2.at[xymod(me2 + j)])

        fin[half] = jnp.sum(rb2[...].astype(F32), axis=0)

        @pl.loop(1, NXY)
        def _(j):
            send(fin.at[half], fin.at[half], sb3.at[j], qb3.at[half], f, xymod(xy + j) * 2 + zl)

    for b in range(8):
        cells = gp[:, 2 * b : 2 * b + 4].reshape(512, 256)
        term = jnp.dot(ta[...], cells, preferred_element_type=F32).reshape(2, 2, 3, 32, 256)
        rows = term[:, :, 1] + shifted(term[:, :, 0], -1) + shifted(term[:, :, 2], 1)
        out_v[:, 2 * b : 2 * b + 2] = rows.astype(BF)

    for x in range(2):
        turned = jnp.swapaxes(out_v[x].astype(F32), 0, 1)
        out_t[:, x] = turned.astype(BF)


    @pl.loop(1, NXY)
    def _(j):
        wait(ra1.at[0], qa1.at[xymod(xy + j)])

    sa[...] = jnp.sum(ra1[...].astype(F32), axis=0).astype(BF)

    for j in FAR_Z:
        t = xymod(me2 + j)
        send(sa, ra2.at[me2], sa2.at[j], qa2.at[me2], t // 2, xy * 2 + lax.rem(t, 2))

    ra2[me2] = sa[...]

    @pl.loop(1, NXY)
    def _(j):
        wait(ra2.at[0], qa2.at[xymod(me2 + j)])

    ra3[xy] = jnp.sum(ra2[...].astype(F32), axis=0).astype(BF)

    for j in FAR_XY:
        k = xymod(xy + j)
        send(ra3.at[xy], ra3.at[xy], sa3.at[j], qa3.at[xy], f, k * 2 + zl)

    for h in range(2):

        @pl.when(xy != 2 * f + h)
        def _():
            wait(fin.at[h], qb3.at[h])

    scale_b = 1.0 / math.sqrt(ns * NF * ROWS * 128)
    scale_a = 1.0 / math.sqrt(8 * ns * NF * ROWS * 128)

    def unfold(full, per, target, scale):
        for dx in range(3):
            for dy in range(3):
                r0 = ((2 - dx) * 3 + 2 - dy) * per
                for dz in range(3):
                    target[9 * dx + 3 * dy + dz] = (
                        full[r0 : r0 + per, dz * 32 : dz * 32 + 32] * scale
                    )

    unfold(fin[...].reshape(96, 128), 8, gwb_out, scale_b)

    @pl.loop(1, NXY)
    def _(j):
        wait(grid_b.at[0, 0], s1.at[j])
        wait(gwb.at[0], sb1.at[j])
        wait(gwa.at[0], sa1.at[j])
        wait(sa, sa2.at[j])

    @pl.loop(0, NXY)
    def _(j):
        wait(grid_b.at[0, 0], sf.at[j])

    @pl.loop(1, 4)
    def _(j):
        wait(wb0, sw.at[j])

    @pl.loop(0, 4)
    def _(j):
        wait(wb0, sx.at[j])

    wait(pool2.at[0], spool.at[0])
    for n, (src, dst, df, dp) in enumerate(pre_moves):
        wait(src, sp.at[n])
    for n, (src, dst, slot, tf, tp) in enumerate(coarse_moves):
        wait(src, sc.at[n])

    for zt in range(2):

        @pl.when((f != owner) | (zl != zt))
        def _():
            wait(sb, sb2.at[zt])

    @pl.when(f == owner)
    def _():
        @pl.loop(1, NXY)
        def _(j):
            wait(fin.at[0], sb3.at[j])


    @pl.loop(1, NXY)
    def _(j):
        wait(ra3.at[0], qa3.at[xymod(xy + j)])

    packed = ra3[...].astype(F32).reshape(256, 128)
    rest = None
    lane = lax.broadcasted_iota(jnp.int32, (72, 128), 1)
    for n in range(3):
        piece = pltpu.roll(packed[n * 72 : n * 72 + 72], 32 * (n + 1), 1)
        rest = piece if n == 0 else jnp.where(lane < 32 * n, rest, piece)
    full = jnp.concatenate([packed[:216], rest], axis=0)
    unfold(full, 32, gwa_out, scale_a)

    @pl.loop(1, NXY)
    def _(j):
        wait(ra3.at[0], sa3.at[j])


def per_device(activation, preact, grad_out, weight_a, weight_b):
    hbm = pl.BlockSpec(memory_space=pltpu.HBM)
    vmem = pl.BlockSpec(memory_space=pltpu.VMEM)
    dma = pltpu.SemaphoreType.DMA
    out, gwa, gwb = pl.pallas_call(
        kernel,
        out_shape=(
            jax.ShapeDtypeStruct((32, 2, 16, 256), BF),
            jax.ShapeDtypeStruct((27, 32, 32), F32),
            jax.ShapeDtypeStruct((27, 8, 32), F32),
        ),
        in_specs=[hbm] * 5,
        out_specs=(vmem,) * 3,
        scratch_shapes=[
            pltpu.VMEM((8, 64, 128), BF),
            pltpu.VMEM((32, 2, 16, 256), BF),
            pltpu.VMEM((32, 2, 16, 256), BF),
            pltpu.VMEM((27, 32, 32), BF),
            pltpu.VMEM((27, 8, 32), BF),
            pltpu.VMEM((528, 128), BF),
            pltpu.VMEM((96, 128), BF),
            pltpu.VMEM((NF, 4, 48, 128), BF),
            pltpu.VMEM((NF, 96, 128), BF),
            pltpu.VMEM((384, 1024), BF),
            pltpu.VMEM((384, 512), BF),
            pltpu.VMEM((4, 18, 32, 256), BF),
            pltpu.VMEM((ROWS, 32, 128), BF),
            pltpu.VMEM((2, 4, 32, 128), BF),
            pltpu.VMEM((512, 256), BF),
            pltpu.VMEM((2, 4, 32, 128), BF),
            pltpu.VMEM((3, 10, 32, 128), BF),
            pltpu.VMEM((4, 18, 32, 256), BF),
            pltpu.VMEM((2, 16, 32, 256), F32),
            pltpu.VMEM((512, 2048), BF),
            pltpu.VMEM((512, 512), F32),
            pltpu.VMEM((2, 16, 32, 256), BF),
            pltpu.VMEM((NXY, 48, 128), BF),
            pltpu.VMEM((NXY, 48, 128), BF),
            pltpu.VMEM((NXY, 48, 128), BF),
            pltpu.VMEM((48, 128), BF),
            pltpu.VMEM((2, 48, 128), F32),
            pltpu.VMEM((NXY, 16, 128), BF),
            pltpu.VMEM((NXY, 16, 128), BF),
            pltpu.VMEM((NXY, 16, 128), BF),
            pltpu.VMEM((NXY, 16, 128), BF),
            pltpu.VMEM((16, 128), BF),
            dma((5,)),
            dma((NXY,)),
            dma((NXY,)),
            dma((NXY,)),
            dma((NXY,)),
            dma((NF,)),
            dma((NF,)),
            dma((4,)),
            dma((1,)),
            dma((1,)),
            dma((8,)),
            dma((8,)),
            dma((7,)),
            dma((7,)),
            dma((NXY,)),
            dma((NXY,)),
            dma((2,)),
            dma((NXY,)),
            dma((NXY,)),
            dma((2,)),
            dma((NXY,)),
            dma((NXY,)),
            dma((NXY,)),
            dma((NXY,)),
            dma((NXY,)),
            dma((NXY,)),
        ],
        compiler_params=pltpu.CompilerParams(
            collective_id=0, has_side_effects=True, vmem_limit_bytes=32 * 1024 * 1024
        ),
    )(
        *(
            pltpu.with_memory_space_constraint(x, pltpu.HBM)
            for x in (grad_out.reshape(8, 64, 128), preact, activation, weight_a, weight_b)
        )
    )
    return (out, gwa, gwb)


def solution(mesh):
    placed = (
        P(None, "space", "filt", None),
        P(None, "space", "filt", None),
        P("filt", "space", None, None),
        P(),
        P(None, "filt", None),
    )
    return jax.shard_map(
        per_device,
        mesh=mesh,
        in_specs=placed,
        out_specs=(P(None, "space", "filt", None), P(), P(None, "filt", None)),
        check_vma=False,
    )
```

```python
import math

import jax
import jax.numpy as jnp
from jax import lax
from jax.experimental import pallas as pl
from jax.experimental.pallas import tpu as pltpu
from jax.sharding import PartitionSpec as P

BF = jnp.bfloat16
F32 = jnp.float32
NF = 8
ROWS = 8
NXY = 16


FAR_XY = (10, 9, 11, 6, 14, 8, 2, 5, 7, 13, 15, 1, 3, 4, 12)
FAR_Z = (8, 7, 9, 6, 10, 5, 11, 4, 12, 3, 13, 14, 15, 1, 2)


def shifted(values, step):
    width = values.shape[-1]
    axis = values.ndim - 1
    lane = lax.broadcasted_iota(jnp.int32, values.shape, axis)
    rolled = pltpu.roll(values, step % width, axis)
    edge = 0 if step == 1 else width - 1
    return jnp.where(lane == edge, 0.0, rolled)


def kernel(
    gout_h,
    pre_h,
    act_h,
    wa_h,
    wb_h,
    out_t,
    gwa_out,
    gwb_out,
    graw,
    praw,
    araw,
    waraw,
    wbraw,
    gsrc,
    wb0,
    grid_b,
    wb_all,
    tb,
    ta,
    prh,
    pool,
    pool2,
    pcat,
    gpo,
    gpc,
    gp,
    actt,
    act3,
    racc,
    out_v,
    gwb,
    rb1,
    rb2,
    sb,
    fin,
    gwa,
    ra1,
    ra2,
    ra3,
    sa,
    sin,
    s1,
    r1,
    sf,
    rf,
    sw,
    rw,
    sx,
    spool,
    rpool,
    sp,
    rp,
    sc,
    rc,
    sb1,
    qb1,
    sb2,
    qb2,
    sb3,
    qb3,
    sa1,
    qa1,
    sa2,
    qa2,
    sa3,
    qa3,
):
    f = lax.axis_index("filt")
    p = lax.axis_index("space")
    ns = lax.axis_size("space")
    xy = p // 2
    zl = p % 2
    me2 = f * 2 + zl

    def fmod(v):
        return lax.rem(v + NF, NF)

    def smod(v):
        return lax.rem(v + ns, ns)

    def xymod(v):
        return lax.rem(v + NXY, NXY)

    def send(src, dst, ss, rs, tf, tp):
        pltpu.make_async_remote_copy(
            src_ref=src,
            dst_ref=dst,
            send_sem=ss,
            recv_sem=rs,
            device_id={"filt": tf, "space": tp},
            device_id_type=pl.DeviceIdType.MESH,
        ).start()

    def wait(ref, sem):
        pltpu.make_async_copy(ref, ref, sem).wait()

    barrier = pltpu.get_barrier_semaphore()

    def greet(tf, tp):
        pl.semaphore_signal(
            barrier,
            inc=1,
            device_id={"filt": tf, "space": tp},
            device_id_type=pl.DeviceIdType.MESH,
        )

    cross = xymod(xy + 2 * zl - 1) * 2 + 1 - zl
    greet(f, cross)
    greet(fmod(f - 1), cross)
    greet(fmod(f + 1), cross)
    greet(fmod(f - 1), xymod(xy + 1) * 2 + zl)
    greet(fmod(f + 1), xymod(xy - 1) * 2 + zl)

    @pl.loop(1, NXY)
    def _(j):
        t = xymod(me2 + j)
        greet(t // 2, xy * 2 + lax.rem(t, 2))

    @pl.loop(1, NXY)
    def _(j):
        greet(f, xymod(xy + j) * 2 + zl)

    loads = [
        pltpu.make_async_copy(src, dst, sin.at[n])
        for n, (src, dst) in enumerate(
            ((gout_h, graw), (wb_h, wbraw), (pre_h, praw), (wa_h, waraw), (act_h, araw))
        )
    ]
    for load in loads:
        load.start()

    def selection(rows, per, high, low):
        row = lax.broadcasted_iota(jnp.int32, (rows, 4 * high), 0)
        col = lax.broadcasted_iota(jnp.int32, (rows, 4 * high), 1)
        tap = lax.shift_right_logical(row, per.bit_length() - 1)
        dx = lax.shift_right_logical(tap * 11, 5)
        dy = tap - 3 * dx
        place = (2 - dx) * high + (2 - dy) * low + (row - tap * per)
        return jnp.where(col == place, 1.0, 0.0).astype(BF)

    def arranged(raw, per, high, low):
        place = selection(9 * per, per, high, low)
        parts = []
        for dz in range(3):
            tall = jnp.concatenate([raw[3 * k + dz].astype(F32) for k in range(9)], axis=0)
            parts.append(
                lax.dot_general(
                    tall.astype(BF),
                    place,
                    (((0,), (0,)), ((), ())),
                    preferred_element_type=F32,
                )
            )
        return jnp.concatenate(parts, axis=0)

    loads[0].wait()
    rows = jnp.swapaxes(graw[...].astype(F32), 0, 1).reshape(512, 128)
    edge = jnp.zeros((8, 128), F32)
    gsrc[...] = jnp.concatenate([edge, rows, edge], axis=0).astype(BF)
    loads[1].wait()
    wb0[...] = arranged(wbraw, 8, 32, 8).astype(BF)

    pl.semaphore_wait(barrier, 2 * (NXY - 1) + 5)

    core = lax.rem(f, 2)
    sibling = f + 1 - 2 * core

    toward = fmod(f + 4 * zl - 2)
    send(wb0, wb_all.at[f], sw.at[1], rw.at[f], fmod(f + 4), xy * 2 + 1 - zl)
    send(wb0, wb_all.at[f], sw.at[2], rw.at[f], toward, p)
    send(wb0, wb_all.at[f], sw.at[3], rw.at[f], toward, xy * 2 + 1 - zl)

    send(wb0, wb_all.at[f], sx.at[0], rw.at[f], sibling, p)
    wb_all[f] = wb0[...]

    def block(t):
        return gsrc.at[pl.ds(pl.multiple_of(t * 32, 16), 48)]

    @pl.loop(1, NXY)
    def _(j):
        t = xymod(me2 + j)
        send(
            block(t),
            grid_b.at[f, 1 + zl],
            s1.at[j],
            r1.at[me2],
            t // 2,
            xy * 2 + lax.rem(t, 2),
        )

    loads[2].wait()
    for x in range(2):
        turned = jnp.swapaxes(praw[:, x].astype(F32), 0, 1)
        prh[1 + x, 1:17] = turned.astype(BF)

    pre_moves = (
        (prh.at[1, pl.ds(1, 16)], prh.at[3, pl.ds(1, 16)], 0, -1),
        (prh.at[2, pl.ds(1, 16)], prh.at[0, pl.ds(1, 16)], 0, 1),
        (prh.at[pl.ds(1, 2), 1], prh.at[pl.ds(1, 2), 17], -1, 0),
        (prh.at[pl.ds(1, 2), 16], prh.at[pl.ds(1, 2), 0], 1, 0),
        (prh.at[1, 1], prh.at[3, 17], -1, -1),
        (prh.at[1, 16], prh.at[3, 0], 1, -1),
        (prh.at[2, 1], prh.at[0, 17], -1, 1),
        (prh.at[2, 16], prh.at[0, 0], 1, 1),
    )

    grid_b[f, 1 + zl] = gsrc[pl.ds(pl.multiple_of(me2 * 32, 16), 48)]

    def forward(s):
        sz = lax.rem(s, 2)
        send(
            grid_b.at[s // 2, 1 + sz],
            grid_b.at[s // 2, 3 - 3 * sz],
            sf.at[s],
            rf.at[s],
            f,
            xymod(xy + 2 * sz - 1) * 2 + zl,
        )

    forward(me2)

    fine_row = lax.broadcasted_iota(jnp.int32, (256, 128), 0)
    fine_col = lax.broadcasted_iota(jnp.int32, (256, 128), 1)
    down = jnp.where(lax.shift_right_logical(fine_row, 1) == fine_col, 1.0, 0.0).astype(BF)
    total = jnp.zeros((ROWS * 32, 128), F32)
    for x2 in range(2):
        relu = jnp.maximum(prh[1 + x2, 1:17], jnp.zeros((), BF)).reshape(ROWS, 2, 32, 256)
        for y2 in range(2):
            total += jnp.dot(
                relu[:, y2].reshape(ROWS * 32, 256), down, preferred_element_type=F32
            )
    pool[...] = (total * 0.125).astype(BF).reshape(ROWS, 32, 128)
    send(
        pool.at[pl.ds(4 - 4 * zl, 4)],
        pool2.at[zl],
        spool.at[0],
        rpool.at[0],
        f,
        xy * 2 + 1 - zl,
    )
    pool2[zl] = pool[pl.ds(4 * zl, 4)]

    for n, (src, dst, df, dp) in enumerate(pre_moves):
        send(src, dst, sp.at[n], rp.at[n], fmod(f + df), smod(p + dp))

    for j in (1, 3, 2):
        s = fmod(f - 2 * j)
        wait(wb0, rw.at[s])
        send(wb_all.at[s], wb_all.at[s], sx.at[j], rw.at[s], sibling, p)

    @pl.loop(1, NXY)
    def _(j):
        s = xymod(me2 - j)
        wait(grid_b.at[0, 0], r1.at[s])
        forward(s)


    loads[3].wait()
    wide_a = arranged(waraw, 32, 128, 32)
    for n, turn in enumerate((0, 32, 128, 160)):
        ta[n * 96 : n * 96 + 96] = (
            pltpu.roll(wide_a, turn, 1) if turn else wide_a
        ).astype(BF)

    @pl.loop(0, 4)
    def _(j):
        wait(wb0, rw.at[2 * j + 1 - core])

    for n in range(NF):
        wide_b = wb_all[n].astype(F32)
        for k, turn in enumerate((0, 8, 32, 40)):
            tb[k * 96 : k * 96 + 96, n * 128 : n * 128 + 128] = (
                pltpu.roll(wide_b, turn, 1) if turn else wide_b
            ).astype(BF)

    @pl.loop(0, NXY)
    def _(j):
        wait(grid_b.at[0, 0], rf.at[j])

    @pl.when(xy == 0)
    def _():
        grid_b[:, 0] = jnp.zeros((NF,) + grid_b.shape[2:], BF)

    @pl.when(xy == NXY - 1)
    def _():
        grid_b[:, 3] = jnp.zeros((NF,) + grid_b.shape[2:], BF)

    g_cat = jnp.concatenate(
        [grid_b[:, :, 16 * b : 16 * b + 32, :].reshape(1024, 128) for b in range(2)], axis=1
    )
    prod = jnp.dot(tb[...], g_cat, preferred_element_type=F32)
    for b in range(2):
        term = prod[:, b * 128 : b * 128 + 128].reshape(2, 2, 3, 32, 128)
        rows = term[:, :, 1] + shifted(term[:, :, 0], -1) + shifted(term[:, :, 2], 1)
        gpo[:, 2 * b : 2 * b + 2] = rows.astype(BF)

    right = xymod(xy + 1) * 2
    left = xymod(xy - 1) * 2 + 1
    step = fmod(f + 2 * zl - 1)
    own_rows = pl.ds(1 + 4 * zl, 4)
    far = 9 - 9 * zl
    both = pl.ds(0, 2)
    coarse_moves = (
        (gpo, gpc.at[pl.ds(zl, 2), own_rows], 0, f, xy * 2 + 1 - zl),
        (gpo.at[1], gpc.at[0, own_rows], 1 + zl, f, right),
        (gpo.at[0], gpc.at[2, own_rows], 1 + zl, f, left),
        (gpo.at[both, 3 * zl], gpc.at[pl.ds(1, 2), far], 3 + zl, step, xy * 2),
        (gpo.at[both, 3 * zl], gpc.at[pl.ds(0, 2), far], 3 + zl, step, xy * 2 + 1),
        (gpo.at[1, 3 * zl], gpc.at[0, far], 5 + zl, step, right),
        (gpo.at[0, 3 * zl], gpc.at[2, far], 5 + zl, step, left),
    )
    for n, (src, dst, slot, tf, tp) in enumerate(coarse_moves):
        send(src, dst, sc.at[n], rc.at[slot], tf, tp)
    gpc[pl.ds(1 - zl, 2), own_rows] = gpo[...]

    wait(pool2.at[0], rpool.at[0])
    mid = pool2[...].reshape(256, 128).astype(F32)
    for k, version in enumerate((shifted(mid, 1), mid, shifted(mid, -1), jnp.zeros_like(mid))):
        version = version.astype(BF).reshape(2, 2, 2, 32, 128)
        for x2 in range(2):
            for b in range(2):
                for y2 in range(2):
                    r0 = (x2 * 2 + y2) * 128 + k * 32
                    pcat[r0 : r0 + 32, b * 128 : b * 128 + 128] = version[x2, b, y2]
    pairs = lax.dot_general(
        g_cat, pcat[...], (((1,), (1,)), ((), ())), preferred_element_type=F32
    ).reshape(NF, 4, 4, 8, 512)
    folded = None
    for x2 in range(2):
        for y2 in range(2):
            c0 = (x2 * 2 + y2) * 128
            term = pairs[:, x2 : x2 + 3, y2 : y2 + 3, :, c0 : c0 + 128]
            folded = term if folded is None else folded + term
    folded = jnp.concatenate(
        [folded.reshape(NF, 72, 128), jnp.zeros((NF, 24, 128), F32)], axis=1
    )
    gwb[...] = folded.astype(BF).reshape(2 * NF, 48, 128)

    @pl.loop(1, NXY)
    def _(j):
        k = xymod(xy + j)
        send(gwb.at[k], rb1.at[xy], sb1.at[j], qb1.at[xy], f, k * 2 + zl)

    rb1[xy] = gwb[xy]

    loads[4].wait()
    for x in range(2):
        actt[x] = jnp.swapaxes(araw[:, x].astype(F32), 0, 1)

    for b in range(8):
        for x2 in range(2):
            for y2 in range(2):
                wide = actt[x2, 2 * b + y2]
                r0, c0 = (x2 * 2 + y2) * 128, b * 256
                act3[r0 : r0 + 32, c0 : c0 + 256] = shifted(wide, 1).astype(BF)
                act3[r0 + 32 : r0 + 64, c0 : c0 + 256] = wide.astype(BF)
                act3[r0 + 64 : r0 + 96, c0 : c0 + 256] = shifted(wide, -1).astype(BF)
                act3[r0 + 96 : r0 + 128, c0 : c0 + 256] = jnp.zeros((32, 256), BF)

    @pl.loop(1, NXY)
    def _(j):
        wait(rb1.at[0], qb1.at[xymod(xy + j)])

    owner = xy // 2
    sb[...] = jnp.sum(rb1[...].astype(F32), axis=0).astype(BF)
    for zt in range(2):

        @pl.when((f != owner) | (zl != zt))
        def _():
            send(sb, rb2.at[me2], sb2.at[zt], qb2.at[me2], owner, xy * 2 + zt)

    wait(gpo, rc.at[0])
    for n in range(2):
        wait(gpo.at[0], rc.at[1 + n])
        wait(gpo.at[both, 0], rc.at[3 + n])
        wait(gpo.at[0, 0], rc.at[5 + n])
    for n, (src, dst, df, dp) in enumerate(pre_moves):
        wait(dst, rp.at[n])

    @pl.when(p == 0)
    def _():
        prh[0] = jnp.zeros(prh.shape[1:], BF)

    @pl.when(p == ns - 1)
    def _():
        prh[3] = jnp.zeros(prh.shape[1:], BF)

    @pl.when(f == 0)
    def _():
        prh[:, 0] = jnp.zeros((4, 32, 256), BF)

    @pl.when(f == NF - 1)
    def _():
        prh[:, 17] = jnp.zeros((4, 32, 256), BF)

    up_row = lax.broadcasted_iota(jnp.int32, (128, 256), 0)
    up_col = lax.broadcasted_iota(jnp.int32, (128, 256), 1)
    up = jnp.where(lax.shift_right_logical(up_col, 1) == up_row, 0.125, 0.0).astype(BF)
    for plane in range(3):
        fine = (
            jnp.dot(gpc[plane].reshape(320, 128), up, preferred_element_type=F32)
            .astype(BF)
            .reshape(10, 32, 256)
        )
        for xh in ((0,), (1, 2), (3,))[plane]:
            for row in range(10):
                for yh in (2 * row - 1, 2 * row):
                    if 0 <= yh <= 17:
                        gp[xh, yh] = jnp.where(
                            prh[xh, yh] > jnp.zeros((), BF), fine[row], jnp.zeros((), BF)
                        )

    cells = jnp.concatenate(
        [gp[:, 2 * b : 2 * b + 4].reshape(512, 256) for b in range(8)], axis=1
    )
    for x2 in range(2):
        r0, c0 = 128 * x2, 256 * x2
        racc[r0 : r0 + 384, c0 : c0 + 256] = lax.dot_general(
            cells[r0 : r0 + 384],
            act3[c0 : c0 + 256],
            (((1,), (1,)), ((), ())),
            preferred_element_type=F32,
        )

    taps = []
    for dx in range(3):
        for dy in range(3):
            term = None
            for x2 in range(2):
                for y2 in range(2):
                    r0 = ((x2 + dx) * 4 + y2 + dy) * 32
                    c0 = (x2 * 2 + y2) * 128
                    piece = racc[r0 : r0 + 32, c0 : c0 + 128]
                    term = piece if term is None else term + piece
            taps.append(term)
    full = jnp.concatenate(taps, axis=0)
    rest = full[216:288]
    tail = jnp.concatenate([pltpu.roll(rest, turn, 1) for turn in (96, 64, 32)], axis=0)
    lane = lax.broadcasted_iota(jnp.int32, (216, 128), 1)
    packed = jnp.where(lane < 96, full[:216], tail)
    packed = jnp.concatenate([packed, jnp.zeros((40, 128), F32)], axis=0)
    gwa[...] = packed.astype(BF).reshape(NXY, 16, 128)

    for j in FAR_XY:
        k = xymod(xy + j)
        send(gwa.at[k], ra1.at[xy], sa1.at[j], qa1.at[xy], f, k * 2 + zl)

    ra1[xy] = gwa[xy]

    half = lax.rem(xy, 2)

    @pl.when(f == owner)
    def _():
        rb2[me2] = sb[...]

        @pl.loop(1, NXY)
        def _(j):
            wait(rb2.at[0], qb2.at[xymod(me2 + j)])

        fin[half] = jnp.sum(rb2[...].astype(F32), axis=0)

        @pl.loop(1, NXY)
        def _(j):
            send(fin.at[half], fin.at[half], sb3.at[j], qb3.at[half], f, xymod(xy + j) * 2 + zl)

    for b in range(8):
        cells = gp[:, 2 * b : 2 * b + 4].reshape(512, 256)
        term = jnp.dot(ta[...], cells, preferred_element_type=F32).reshape(2, 2, 3, 32, 256)
        rows = term[:, :, 1] + shifted(term[:, :, 0], -1) + shifted(term[:, :, 2], 1)
        out_v[:, 2 * b : 2 * b + 2] = rows.astype(BF)

    for x in range(2):
        turned = jnp.swapaxes(out_v[x].astype(F32), 0, 1)
        out_t[:, x] = turned.astype(BF)


    @pl.loop(1, NXY)
    def _(j):
        wait(ra1.at[0], qa1.at[xymod(xy + j)])

    sa[...] = jnp.sum(ra1[...].astype(F32), axis=0).astype(BF)

    for j in FAR_Z:
        t = xymod(me2 + j)
        send(sa, ra2.at[me2], sa2.at[j], qa2.at[me2], t // 2, xy * 2 + lax.rem(t, 2))

    ra2[me2] = sa[...]

    @pl.loop(1, NXY)
    def _(j):
        wait(ra2.at[0], qa2.at[xymod(me2 + j)])

    ra3[xy] = jnp.sum(ra2[...].astype(F32), axis=0).astype(BF)

    for j in FAR_XY:
        k = xymod(xy + j)
        send(ra3.at[xy], ra3.at[xy], sa3.at[j], qa3.at[xy], f, k * 2 + zl)

    for h in range(2):

        @pl.when(xy != 2 * f + h)
        def _():
            wait(fin.at[h], qb3.at[h])

    scale_b = 1.0 / math.sqrt(ns * NF * ROWS * 128)
    scale_a = 1.0 / math.sqrt(8 * ns * NF * ROWS * 128)

    def unfold(full, per, target, scale):
        for dx in range(3):
            for dy in range(3):
                r0 = ((2 - dx) * 3 + 2 - dy) * per
                for dz in range(3):
                    target[9 * dx + 3 * dy + dz] = (
                        full[r0 : r0 + per, dz * 32 : dz * 32 + 32] * scale
                    )

    unfold(fin[...].reshape(96, 128), 8, gwb_out, scale_b)

    @pl.loop(1, NXY)
    def _(j):
        wait(grid_b.at[0, 0], s1.at[j])
        wait(gwb.at[0], sb1.at[j])
        wait(gwa.at[0], sa1.at[j])
        wait(sa, sa2.at[j])

    @pl.loop(0, NXY)
    def _(j):
        wait(grid_b.at[0, 0], sf.at[j])

    @pl.loop(1, 4)
    def _(j):
        wait(wb0, sw.at[j])

    @pl.loop(0, 4)
    def _(j):
        wait(wb0, sx.at[j])

    wait(pool2.at[0], spool.at[0])
    for n, (src, dst, df, dp) in enumerate(pre_moves):
        wait(src, sp.at[n])
    for n, (src, dst, slot, tf, tp) in enumerate(coarse_moves):
        wait(src, sc.at[n])

    for zt in range(2):

        @pl.when((f != owner) | (zl != zt))
        def _():
            wait(sb, sb2.at[zt])

    @pl.when(f == owner)
    def _():
        @pl.loop(1, NXY)
        def _(j):
            wait(fin.at[0], sb3.at[j])


    @pl.loop(1, NXY)
    def _(j):
        wait(ra3.at[0], qa3.at[xymod(xy + j)])

    packed = ra3[...].astype(F32).reshape(256, 128)
    rest = None
    lane = lax.broadcasted_iota(jnp.int32, (72, 128), 1)
    for n in range(3):
        piece = pltpu.roll(packed[n * 72 : n * 72 + 72], 32 * (n + 1), 1)
        rest = piece if n == 0 else jnp.where(lane < 32 * n, rest, piece)
    full = jnp.concatenate([packed[:216], rest], axis=0)
    unfold(full, 32, gwa_out, scale_a)

    @pl.loop(1, NXY)
    def _(j):
        wait(ra3.at[0], sa3.at[j])


def per_device(activation, preact, grad_out, weight_a, weight_b):
    hbm = pl.BlockSpec(memory_space=pltpu.HBM)
    vmem = pl.BlockSpec(memory_space=pltpu.VMEM)
    dma = pltpu.SemaphoreType.DMA
    out, gwa, gwb = pl.pallas_call(
        kernel,
        out_shape=(
            jax.ShapeDtypeStruct((32, 2, 16, 256), BF),
            jax.ShapeDtypeStruct((27, 32, 32), F32),
            jax.ShapeDtypeStruct((27, 8, 32), F32),
        ),
        in_specs=[hbm] * 5,
        out_specs=(vmem,) * 3,
        scratch_shapes=[
            pltpu.VMEM((8, 64, 128), BF),
            pltpu.VMEM((32, 2, 16, 256), BF),
            pltpu.VMEM((32, 2, 16, 256), BF),
            pltpu.VMEM((27, 32, 32), BF),
            pltpu.VMEM((27, 8, 32), BF),
            pltpu.VMEM((528, 128), BF),
            pltpu.VMEM((96, 128), BF),
            pltpu.VMEM((NF, 4, 48, 128), BF),
            pltpu.VMEM((NF, 96, 128), BF),
            pltpu.VMEM((384, 1024), BF),
            pltpu.VMEM((384, 512), BF),
            pltpu.VMEM((4, 18, 32, 256), BF),
            pltpu.VMEM((ROWS, 32, 128), BF),
            pltpu.VMEM((2, 4, 32, 128), BF),
            pltpu.VMEM((512, 256), BF),
            pltpu.VMEM((2, 4, 32, 128), BF),
            pltpu.VMEM((3, 10, 32, 128), BF),
            pltpu.VMEM((4, 18, 32, 256), BF),
            pltpu.VMEM((2, 16, 32, 256), F32),
            pltpu.VMEM((512, 2048), BF),
            pltpu.VMEM((512, 512), F32),
            pltpu.VMEM((2, 16, 32, 256), BF),
            pltpu.VMEM((NXY, 48, 128), BF),
            pltpu.VMEM((NXY, 48, 128), BF),
            pltpu.VMEM((NXY, 48, 128), BF),
            pltpu.VMEM((48, 128), BF),
            pltpu.VMEM((2, 48, 128), F32),
            pltpu.VMEM((NXY, 16, 128), BF),
            pltpu.VMEM((NXY, 16, 128), BF),
            pltpu.VMEM((NXY, 16, 128), BF),
            pltpu.VMEM((NXY, 16, 128), BF),
            pltpu.VMEM((16, 128), BF),
            dma((5,)),
            dma((NXY,)),
            dma((NXY,)),
            dma((NXY,)),
            dma((NXY,)),
            dma((NF,)),
            dma((NF,)),
            dma((4,)),
            dma((1,)),
            dma((1,)),
            dma((8,)),
            dma((8,)),
            dma((7,)),
            dma((7,)),
            dma((NXY,)),
            dma((NXY,)),
            dma((2,)),
            dma((NXY,)),
            dma((NXY,)),
            dma((2,)),
            dma((NXY,)),
            dma((NXY,)),
            dma((NXY,)),
            dma((NXY,)),
            dma((NXY,)),
            dma((NXY,)),
        ],
        compiler_params=pltpu.CompilerParams(
            collective_id=0, has_side_effects=True, vmem_limit_bytes=32 * 1024 * 1024
        ),
    )(
        *(
            pltpu.with_memory_space_constraint(x, pltpu.HBM)
            for x in (grad_out.reshape(8, 64, 128), preact, activation, weight_a, weight_b)
        )
    )
    return (out, gwa, gwb)


def solution(mesh):
    placed = (
        P(None, "space", "filt", None),
        P(None, "space", "filt", None),
        P("filt", "space", None, None),
        P(),
        P(None, "filt", None),
    )
    return jax.shard_map(
        per_device,
        mesh=mesh,
        in_specs=placed,
        out_specs=(P(None, "space", "filt", None), P(), P(None, "filt", None)),
        check_vma=False,
    )
```

```python
import math

import jax
import jax.numpy as jnp
from jax import lax
from jax.experimental import pallas as pl
from jax.experimental.pallas import tpu as pltpu
from jax.sharding import PartitionSpec as P

BF = jnp.bfloat16
F32 = jnp.float32
NF = 8
ROWS = 8
NXY = 16


FAR_XY = (10, 9, 11, 6, 14, 8, 2, 5, 7, 13, 15, 1, 3, 4, 12)
FAR_Z = (8, 7, 9, 6, 10, 5, 11, 4, 12, 3, 13, 14, 15, 1, 2)


def shifted(values, step):
    width = values.shape[-1]
    axis = values.ndim - 1
    lane = lax.broadcasted_iota(jnp.int32, values.shape, axis)
    rolled = pltpu.roll(values, step % width, axis)
    edge = 0 if step == 1 else width - 1
    return jnp.where(lane == edge, 0.0, rolled)


def kernel(
    gout_h,
    pre_h,
    act_h,
    wa_h,
    wb_h,
    out_t,
    gwa_out,
    gwb_out,
    graw,
    praw,
    araw,
    waraw,
    wbraw,
    gsrc,
    wb0,
    grid_b,
    wb_all,
    tb,
    ta,
    prh,
    pool,
    pool2,
    pcat,
    gpo,
    gpc,
    gp,
    actt,
    act3,
    racc,
    out_v,
    gwb,
    rb1,
    rb2,
    sb,
    fin,
    gwa,
    ra1,
    ra2,
    ra3,
    sa,
    sin,
    s1,
    r1,
    sf,
    rf,
    sw,
    rw,
    sx,
    spool,
    rpool,
    sp,
    rp,
    sc,
    rc,
    sb1,
    qb1,
    sb2,
    qb2,
    sb3,
    qb3,
    sa1,
    qa1,
    sa2,
    qa2,
    sa3,
    qa3,
):
    f = lax.axis_index("filt")
    p = lax.axis_index("space")
    ns = lax.axis_size("space")
    xy = p // 2
    zl = p % 2
    me2 = f * 2 + zl

    def fmod(v):
        return lax.rem(v + NF, NF)

    def smod(v):
        return lax.rem(v + ns, ns)

    def xymod(v):
        return lax.rem(v + NXY, NXY)

    def send(src, dst, ss, rs, tf, tp):
        pltpu.make_async_remote_copy(
            src_ref=src,
            dst_ref=dst,
            send_sem=ss,
            recv_sem=rs,
            device_id={"filt": tf, "space": tp},
            device_id_type=pl.DeviceIdType.MESH,
        ).start()

    def wait(ref, sem):
        pltpu.make_async_copy(ref, ref, sem).wait()

    barrier = pltpu.get_barrier_semaphore()

    def greet(tf, tp):
        pl.semaphore_signal(
            barrier,
            inc=1,
            device_id={"filt": tf, "space": tp},
            device_id_type=pl.DeviceIdType.MESH,
        )

    cross = xymod(xy + 2 * zl - 1) * 2 + 1 - zl
    greet(f, cross)
    greet(fmod(f - 1), cross)
    greet(fmod(f + 1), cross)
    greet(fmod(f - 1), xymod(xy + 1) * 2 + zl)
    greet(fmod(f + 1), xymod(xy - 1) * 2 + zl)

    @pl.loop(1, NXY)
    def _(j):
        t = xymod(me2 + j)
        greet(t // 2, xy * 2 + lax.rem(t, 2))

    @pl.loop(1, NXY)
    def _(j):
        greet(f, xymod(xy + j) * 2 + zl)

    loads = [
        pltpu.make_async_copy(src, dst, sin.at[n])
        for n, (src, dst) in enumerate(
            ((gout_h, graw), (wb_h, wbraw), (pre_h, praw), (wa_h, waraw), (act_h, araw))
        )
    ]
    for load in loads:
        load.start()

    def selection(rows, per, high, low):
        row = lax.broadcasted_iota(jnp.int32, (rows, 4 * high), 0)
        col = lax.broadcasted_iota(jnp.int32, (rows, 4 * high), 1)
        tap = lax.shift_right_logical(row, per.bit_length() - 1)
        dx = lax.shift_right_logical(tap * 11, 5)
        dy = tap - 3 * dx
        place = (2 - dx) * high + (2 - dy) * low + (row - tap * per)
        return jnp.where(col == place, 1.0, 0.0).astype(BF)

    def arranged(raw, per, high, low):
        place = selection(9 * per, per, high, low)
        parts = []
        for dz in range(3):
            tall = jnp.concatenate([raw[3 * k + dz].astype(F32) for k in range(9)], axis=0)
            parts.append(
                lax.dot_general(
                    tall.astype(BF),
                    place,
                    (((0,), (0,)), ((), ())),
                    preferred_element_type=F32,
                )
            )
        return jnp.concatenate(parts, axis=0)

    loads[0].wait()
    rows = jnp.swapaxes(graw[...].astype(F32), 0, 1).reshape(512, 128)
    edge = jnp.zeros((8, 128), F32)
    gsrc[...] = jnp.concatenate([edge, rows, edge], axis=0).astype(BF)
    loads[1].wait()
    wb0[...] = arranged(wbraw, 8, 32, 8).astype(BF)

    pl.semaphore_wait(barrier, 2 * (NXY - 1) + 5)

    core = lax.rem(f, 2)
    sibling = f + 1 - 2 * core

    toward = fmod(f + 4 * zl - 2)
    send(wb0, wb_all.at[f], sw.at[1], rw.at[f], fmod(f + 4), xy * 2 + 1 - zl)
    send(wb0, wb_all.at[f], sw.at[2], rw.at[f], toward, p)
    send(wb0, wb_all.at[f], sw.at[3], rw.at[f], toward, xy * 2 + 1 - zl)

    send(wb0, wb_all.at[f], sx.at[0], rw.at[f], sibling, p)
    wb_all[f] = wb0[...]

    def block(t):
        return gsrc.at[pl.ds(pl.multiple_of(t * 32, 16), 48)]

    @pl.loop(1, NXY)
    def _(j):
        t = xymod(me2 + j)
        send(
            block(t),
            grid_b.at[f, 1 + zl],
            s1.at[j],
            r1.at[me2],
            t // 2,
            xy * 2 + lax.rem(t, 2),
        )

    loads[2].wait()
    for x in range(2):
        turned = jnp.swapaxes(praw[:, x].astype(F32), 0, 1)
        prh[1 + x, 1:17] = turned.astype(BF)

    pre_moves = (
        (prh.at[1, pl.ds(1, 16)], prh.at[3, pl.ds(1, 16)], 0, -1),
        (prh.at[2, pl.ds(1, 16)], prh.at[0, pl.ds(1, 16)], 0, 1),
        (prh.at[pl.ds(1, 2), 1], prh.at[pl.ds(1, 2), 17], -1, 0),
        (prh.at[pl.ds(1, 2), 16], prh.at[pl.ds(1, 2), 0], 1, 0),
        (prh.at[1, 1], prh.at[3, 17], -1, -1),
        (prh.at[1, 16], prh.at[3, 0], 1, -1),
        (prh.at[2, 1], prh.at[0, 17], -1, 1),
        (prh.at[2, 16], prh.at[0, 0], 1, 1),
    )

    grid_b[f, 1 + zl] = gsrc[pl.ds(pl.multiple_of(me2 * 32, 16), 48)]

    def forward(s):
        sz = lax.rem(s, 2)
        send(
            grid_b.at[s // 2, 1 + sz],
            grid_b.at[s // 2, 3 - 3 * sz],
            sf.at[s],
            rf.at[s],
            f,
            xymod(xy + 2 * sz - 1) * 2 + zl,
        )

    forward(me2)

    fine_row = lax.broadcasted_iota(jnp.int32, (256, 128), 0)
    fine_col = lax.broadcasted_iota(jnp.int32, (256, 128), 1)
    down = jnp.where(lax.shift_right_logical(fine_row, 1) == fine_col, 1.0, 0.0).astype(BF)
    total = jnp.zeros((ROWS * 32, 128), F32)
    for x2 in range(2):
        relu = jnp.maximum(prh[1 + x2, 1:17], jnp.zeros((), BF)).reshape(ROWS, 2, 32, 256)
        for y2 in range(2):
            total += jnp.dot(
                relu[:, y2].reshape(ROWS * 32, 256), down, preferred_element_type=F32
            )
    pool[...] = (total * 0.125).astype(BF).reshape(ROWS, 32, 128)
    send(
        pool.at[pl.ds(4 - 4 * zl, 4)],
        pool2.at[zl],
        spool.at[0],
        rpool.at[0],
        f,
        xy * 2 + 1 - zl,
    )
    pool2[zl] = pool[pl.ds(4 * zl, 4)]

    for n, (src, dst, df, dp) in enumerate(pre_moves):
        send(src, dst, sp.at[n], rp.at[n], fmod(f + df), smod(p + dp))

    for j in (1, 3, 2):
        s = fmod(f - 2 * j)
        wait(wb0, rw.at[s])
        send(wb_all.at[s], wb_all.at[s], sx.at[j], rw.at[s], sibling, p)

    @pl.loop(1, NXY)
    def _(j):
        s = xymod(me2 - j)
        wait(grid_b.at[0, 0], r1.at[s])
        forward(s)


    loads[3].wait()
    wide_a = arranged(waraw, 32, 128, 32)
    for n, turn in enumerate((0, 32, 128, 160)):
        ta[n * 96 : n * 96 + 96] = (
            pltpu.roll(wide_a, turn, 1) if turn else wide_a
        ).astype(BF)

    @pl.loop(0, 4)
    def _(j):
        wait(wb0, rw.at[2 * j + 1 - core])

    for n in range(NF):
        wide_b = wb_all[n].astype(F32)
        for k, turn in enumerate((0, 8, 32, 40)):
            tb[k * 96 : k * 96 + 96, n * 128 : n * 128 + 128] = (
                pltpu.roll(wide_b, turn, 1) if turn else wide_b
            ).astype(BF)

    @pl.loop(0, NXY)
    def _(j):
        wait(grid_b.at[0, 0], rf.at[j])

    @pl.when(xy == 0)
    def _():
        grid_b[:, 0] = jnp.zeros((NF,) + grid_b.shape[2:], BF)

    @pl.when(xy == NXY - 1)
    def _():
        grid_b[:, 3] = jnp.zeros((NF,) + grid_b.shape[2:], BF)

    g_cat = jnp.concatenate(
        [grid_b[:, :, 16 * b : 16 * b + 32, :].reshape(1024, 128) for b in range(2)], axis=1
    )
    prod = jnp.dot(tb[...], g_cat, preferred_element_type=F32)
    for b in range(2):
        term = prod[:, b * 128 : b * 128 + 128].reshape(2, 2, 3, 32, 128)
        rows = term[:, :, 1] + shifted(term[:, :, 0], -1) + shifted(term[:, :, 2], 1)
        gpo[:, 2 * b : 2 * b + 2] = rows.astype(BF)

    right = xymod(xy + 1) * 2
    left = xymod(xy - 1) * 2 + 1
    step = fmod(f + 2 * zl - 1)
    own_rows = pl.ds(1 + 4 * zl, 4)
    far = 9 - 9 * zl
    both = pl.ds(0, 2)
    coarse_moves = (
        (gpo, gpc.at[pl.ds(zl, 2), own_rows], 0, f, xy * 2 + 1 - zl),
        (gpo.at[1], gpc.at[0, own_rows], 1 + zl, f, right),
        (gpo.at[0], gpc.at[2, own_rows], 1 + zl, f, left),
        (gpo.at[both, 3 * zl], gpc.at[pl.ds(1, 2), far], 3 + zl, step, xy * 2),
        (gpo.at[both, 3 * zl], gpc.at[pl.ds(0, 2), far], 3 + zl, step, xy * 2 + 1),
        (gpo.at[1, 3 * zl], gpc.at[0, far], 5 + zl, step, right),
        (gpo.at[0, 3 * zl], gpc.at[2, far], 5 + zl, step, left),
    )
    for n, (src, dst, slot, tf, tp) in enumerate(coarse_moves):
        send(src, dst, sc.at[n], rc.at[slot], tf, tp)
    gpc[pl.ds(1 - zl, 2), own_rows] = gpo[...]

    wait(pool2.at[0], rpool.at[0])
    mid = pool2[...].reshape(256, 128).astype(F32)
    for k, version in enumerate((shifted(mid, 1), mid, shifted(mid, -1), jnp.zeros_like(mid))):
        version = version.astype(BF).reshape(2, 2, 2, 32, 128)
        for x2 in range(2):
            for b in range(2):
                for y2 in range(2):
                    r0 = (x2 * 2 + y2) * 128 + k * 32
                    pcat[r0 : r0 + 32, b * 128 : b * 128 + 128] = version[x2, b, y2]
    pairs = lax.dot_general(
        g_cat, pcat[...], (((1,), (1,)), ((), ())), preferred_element_type=F32
    ).reshape(NF, 4, 4, 8, 512)
    folded = None
    for x2 in range(2):
        for y2 in range(2):
            c0 = (x2 * 2 + y2) * 128
            term = pairs[:, x2 : x2 + 3, y2 : y2 + 3, :, c0 : c0 + 128]
            folded = term if folded is None else folded + term
    folded = jnp.concatenate(
        [folded.reshape(NF, 72, 128), jnp.zeros((NF, 24, 128), F32)], axis=1
    )
    gwb[...] = folded.astype(BF).reshape(2 * NF, 48, 128)

    @pl.loop(1, NXY)
    def _(j):
        k = xymod(xy + j)
        send(gwb.at[k], rb1.at[xy], sb1.at[j], qb1.at[xy], f, k * 2 + zl)

    rb1[xy] = gwb[xy]

    loads[4].wait()
    for x in range(2):
        actt[x] = jnp.swapaxes(araw[:, x].astype(F32), 0, 1)

    for b in range(8):
        for x2 in range(2):
            for y2 in range(2):
                wide = actt[x2, 2 * b + y2]
                r0, c0 = (x2 * 2 + y2) * 128, b * 256
                act3[r0 : r0 + 32, c0 : c0 + 256] = shifted(wide, 1).astype(BF)
                act3[r0 + 32 : r0 + 64, c0 : c0 + 256] = wide.astype(BF)
                act3[r0 + 64 : r0 + 96, c0 : c0 + 256] = shifted(wide, -1).astype(BF)
                act3[r0 + 96 : r0 + 128, c0 : c0 + 256] = jnp.zeros((32, 256), BF)

    wait(gpo, rc.at[0])
    for n in range(2):
        wait(gpo.at[0], rc.at[1 + n])
        wait(gpo.at[both, 0], rc.at[3 + n])
        wait(gpo.at[0, 0], rc.at[5 + n])
    for n, (src, dst, df, dp) in enumerate(pre_moves):
        wait(dst, rp.at[n])

    @pl.when(p == 0)
    def _():
        prh[0] = jnp.zeros(prh.shape[1:], BF)

    @pl.when(p == ns - 1)
    def _():
        prh[3] = jnp.zeros(prh.shape[1:], BF)

    @pl.when(f == 0)
    def _():
        prh[:, 0] = jnp.zeros((4, 32, 256), BF)

    @pl.when(f == NF - 1)
    def _():
        prh[:, 17] = jnp.zeros((4, 32, 256), BF)

    up_row = lax.broadcasted_iota(jnp.int32, (128, 256), 0)
    up_col = lax.broadcasted_iota(jnp.int32, (128, 256), 1)
    up = jnp.where(lax.shift_right_logical(up_col, 1) == up_row, 0.125, 0.0).astype(BF)
    for plane in range(3):
        fine = (
            jnp.dot(gpc[plane].reshape(320, 128), up, preferred_element_type=F32)
            .astype(BF)
            .reshape(10, 32, 256)
        )
        for xh in ((0,), (1, 2), (3,))[plane]:
            for row in range(10):
                for yh in (2 * row - 1, 2 * row):
                    if 0 <= yh <= 17:
                        gp[xh, yh] = jnp.where(
                            prh[xh, yh] > jnp.zeros((), BF), fine[row], jnp.zeros((), BF)
                        )

    cells = jnp.concatenate(
        [gp[:, 2 * b : 2 * b + 4].reshape(512, 256) for b in range(8)], axis=1
    )
    for x2 in range(2):
        r0, c0 = 128 * x2, 256 * x2
        racc[r0 : r0 + 384, c0 : c0 + 256] = lax.dot_general(
            cells[r0 : r0 + 384],
            act3[c0 : c0 + 256],
            (((1,), (1,)), ((), ())),
            preferred_element_type=F32,
        )

    taps = []
    for dx in range(3):
        for dy in range(3):
            term = None
            for x2 in range(2):
                for y2 in range(2):
                    r0 = ((x2 + dx) * 4 + y2 + dy) * 32
                    c0 = (x2 * 2 + y2) * 128
                    piece = racc[r0 : r0 + 32, c0 : c0 + 128]
                    term = piece if term is None else term + piece
            taps.append(term)
    full = jnp.concatenate(taps, axis=0)
    rest = full[216:288]
    tail = jnp.concatenate([pltpu.roll(rest, turn, 1) for turn in (96, 64, 32)], axis=0)
    lane = lax.broadcasted_iota(jnp.int32, (216, 128), 1)
    packed = jnp.where(lane < 96, full[:216], tail)
    packed = jnp.concatenate([packed, jnp.zeros((40, 128), F32)], axis=0)
    gwa[...] = packed.astype(BF).reshape(NXY, 16, 128)

    for j in FAR_XY:
        k = xymod(xy + j)
        send(gwa.at[k], ra1.at[xy], sa1.at[j], qa1.at[xy], f, k * 2 + zl)

    ra1[xy] = gwa[xy]

    @pl.loop(1, NXY)
    def _(j):
        wait(rb1.at[0], qb1.at[xymod(xy + j)])

    owner = xy // 2
    sb[...] = jnp.sum(rb1[...].astype(F32), axis=0).astype(BF)
    for zt in range(2):

        @pl.when((f != owner) | (zl != zt))
        def _():
            send(sb, rb2.at[me2], sb2.at[zt], qb2.at[me2], owner, xy * 2 + zt)

    for b in range(8):
        cells = gp[:, 2 * b : 2 * b + 4].reshape(512, 256)
        term = jnp.dot(ta[...], cells, preferred_element_type=F32).reshape(2, 2, 3, 32, 256)
        rows = term[:, :, 1] + shifted(term[:, :, 0], -1) + shifted(term[:, :, 2], 1)
        out_v[:, 2 * b : 2 * b + 2] = rows.astype(BF)

    for x in range(2):
        turned = jnp.swapaxes(out_v[x].astype(F32), 0, 1)
        out_t[:, x] = turned.astype(BF)


    @pl.loop(1, NXY)
    def _(j):
        wait(ra1.at[0], qa1.at[xymod(xy + j)])

    sa[...] = jnp.sum(ra1[...].astype(F32), axis=0).astype(BF)

    for j in FAR_Z:
        t = xymod(me2 + j)
        send(sa, ra2.at[me2], sa2.at[j], qa2.at[me2], t // 2, xy * 2 + lax.rem(t, 2))

    ra2[me2] = sa[...]

    half = lax.rem(xy, 2)

    @pl.when(f == owner)
    def _():
        rb2[me2] = sb[...]

        @pl.loop(1, NXY)
        def _(j):
            wait(rb2.at[0], qb2.at[xymod(me2 + j)])

        fin[half] = jnp.sum(rb2[...].astype(F32), axis=0)

        @pl.loop(1, NXY)
        def _(j):
            send(fin.at[half], fin.at[half], sb3.at[j], qb3.at[half], f, xymod(xy + j) * 2 + zl)

    @pl.loop(1, NXY)
    def _(j):
        wait(ra2.at[0], qa2.at[xymod(me2 + j)])

    ra3[xy] = jnp.sum(ra2[...].astype(F32), axis=0).astype(BF)

    for j in FAR_XY:
        k = xymod(xy + j)
        send(ra3.at[xy], ra3.at[xy], sa3.at[j], qa3.at[xy], f, k * 2 + zl)

    for h in range(2):

        @pl.when(xy != 2 * f + h)
        def _():
            wait(fin.at[h], qb3.at[h])

    scale_b = 1.0 / math.sqrt(ns * NF * ROWS * 128)
    scale_a = 1.0 / math.sqrt(8 * ns * NF * ROWS * 128)

    def unfold(full, per, target, scale):
        for dx in range(3):
            for dy in range(3):
                r0 = ((2 - dx) * 3 + 2 - dy) * per
                for dz in range(3):
                    target[9 * dx + 3 * dy + dz] = (
                        full[r0 : r0 + per, dz * 32 : dz * 32 + 32] * scale
                    )

    unfold(fin[...].reshape(96, 128), 8, gwb_out, scale_b)

    @pl.loop(1, NXY)
    def _(j):
        wait(grid_b.at[0, 0], s1.at[j])
        wait(gwb.at[0], sb1.at[j])
        wait(gwa.at[0], sa1.at[j])
        wait(sa, sa2.at[j])

    @pl.loop(0, NXY)
    def _(j):
        wait(grid_b.at[0, 0], sf.at[j])

    @pl.loop(1, 4)
    def _(j):
        wait(wb0, sw.at[j])

    @pl.loop(0, 4)
    def _(j):
        wait(wb0, sx.at[j])

    wait(pool2.at[0], spool.at[0])
    for n, (src, dst, df, dp) in enumerate(pre_moves):
        wait(src, sp.at[n])
    for n, (src, dst, slot, tf, tp) in enumerate(coarse_moves):
        wait(src, sc.at[n])

    for zt in range(2):

        @pl.when((f != owner) | (zl != zt))
        def _():
            wait(sb, sb2.at[zt])

    @pl.when(f == owner)
    def _():
        @pl.loop(1, NXY)
        def _(j):
            wait(fin.at[0], sb3.at[j])


    @pl.loop(1, NXY)
    def _(j):
        wait(ra3.at[0], qa3.at[xymod(xy + j)])

    packed = ra3[...].astype(F32).reshape(256, 128)
    rest = None
    lane = lax.broadcasted_iota(jnp.int32, (72, 128), 1)
    for n in range(3):
        piece = pltpu.roll(packed[n * 72 : n * 72 + 72], 32 * (n + 1), 1)
        rest = piece if n == 0 else jnp.where(lane < 32 * n, rest, piece)
    full = jnp.concatenate([packed[:216], rest], axis=0)
    unfold(full, 32, gwa_out, scale_a)

    @pl.loop(1, NXY)
    def _(j):
        wait(ra3.at[0], sa3.at[j])


def per_device(activation, preact, grad_out, weight_a, weight_b):
    hbm = pl.BlockSpec(memory_space=pltpu.HBM)
    vmem = pl.BlockSpec(memory_space=pltpu.VMEM)
    dma = pltpu.SemaphoreType.DMA
    out, gwa, gwb = pl.pallas_call(
        kernel,
        out_shape=(
            jax.ShapeDtypeStruct((32, 2, 16, 256), BF),
            jax.ShapeDtypeStruct((27, 32, 32), F32),
            jax.ShapeDtypeStruct((27, 8, 32), F32),
        ),
        in_specs=[hbm] * 5,
        out_specs=(vmem,) * 3,
        scratch_shapes=[
            pltpu.VMEM((8, 64, 128), BF),
            pltpu.VMEM((32, 2, 16, 256), BF),
            pltpu.VMEM((32, 2, 16, 256), BF),
            pltpu.VMEM((27, 32, 32), BF),
            pltpu.VMEM((27, 8, 32), BF),
            pltpu.VMEM((528, 128), BF),
            pltpu.VMEM((96, 128), BF),
            pltpu.VMEM((NF, 4, 48, 128), BF),
            pltpu.VMEM((NF, 96, 128), BF),
            pltpu.VMEM((384, 1024), BF),
            pltpu.VMEM((384, 512), BF),
            pltpu.VMEM((4, 18, 32, 256), BF),
            pltpu.VMEM((ROWS, 32, 128), BF),
            pltpu.VMEM((2, 4, 32, 128), BF),
            pltpu.VMEM((512, 256), BF),
            pltpu.VMEM((2, 4, 32, 128), BF),
            pltpu.VMEM((3, 10, 32, 128), BF),
            pltpu.VMEM((4, 18, 32, 256), BF),
            pltpu.VMEM((2, 16, 32, 256), F32),
            pltpu.VMEM((512, 2048), BF),
            pltpu.VMEM((512, 512), F32),
            pltpu.VMEM((2, 16, 32, 256), BF),
            pltpu.VMEM((NXY, 48, 128), BF),
            pltpu.VMEM((NXY, 48, 128), BF),
            pltpu.VMEM((NXY, 48, 128), BF),
            pltpu.VMEM((48, 128), BF),
            pltpu.VMEM((2, 48, 128), F32),
            pltpu.VMEM((NXY, 16, 128), BF),
            pltpu.VMEM((NXY, 16, 128), BF),
            pltpu.VMEM((NXY, 16, 128), BF),
            pltpu.VMEM((NXY, 16, 128), BF),
            pltpu.VMEM((16, 128), BF),
            dma((5,)),
            dma((NXY,)),
            dma((NXY,)),
            dma((NXY,)),
            dma((NXY,)),
            dma((NF,)),
            dma((NF,)),
            dma((4,)),
            dma((1,)),
            dma((1,)),
            dma((8,)),
            dma((8,)),
            dma((7,)),
            dma((7,)),
            dma((NXY,)),
            dma((NXY,)),
            dma((2,)),
            dma((NXY,)),
            dma((NXY,)),
            dma((2,)),
            dma((NXY,)),
            dma((NXY,)),
            dma((NXY,)),
            dma((NXY,)),
            dma((NXY,)),
            dma((NXY,)),
        ],
        compiler_params=pltpu.CompilerParams(
            collective_id=0, has_side_effects=True, vmem_limit_bytes=32 * 1024 * 1024
        ),
    )(
        *(
            pltpu.with_memory_space_constraint(x, pltpu.HBM)
            for x in (grad_out.reshape(8, 64, 128), preact, activation, weight_a, weight_b)
        )
    )
    return (out, gwa, gwb)


def solution(mesh):
    placed = (
        P(None, "space", "filt", None),
        P(None, "space", "filt", None),
        P("filt", "space", None, None),
        P(),
        P(None, "filt", None),
    )
    return jax.shard_map(
        per_device,
        mesh=mesh,
        in_specs=placed,
        out_specs=(P(None, "space", "filt", None), P(), P(None, "filt", None)),
        check_vma=False,
    )
```

```python
import math

import jax
import jax.numpy as jnp
from jax import lax
from jax.experimental import pallas as pl
from jax.experimental.pallas import tpu as pltpu
from jax.sharding import PartitionSpec as P

BF = jnp.bfloat16
F32 = jnp.float32
NF = 8
ROWS = 8
NXY = 16


FAR_XY = (10, 9, 11, 6, 14, 8, 2, 5, 7, 13, 15, 1, 3, 4, 12)
FAR_Z = (8, 7, 9, 6, 10, 5, 11, 4, 12, 3, 13, 14, 15, 1, 2)


def shifted(values, step):
    width = values.shape[-1]
    axis = values.ndim - 1
    lane = lax.broadcasted_iota(jnp.int32, values.shape, axis)
    rolled = pltpu.roll(values, step % width, axis)
    edge = 0 if step == 1 else width - 1
    return jnp.where(lane == edge, 0.0, rolled)


def kernel(
    gout_h,
    pre_h,
    act_h,
    wa_h,
    wb_h,
    out_t,
    gwa_out,
    gwb_out,
    graw,
    praw,
    araw,
    waraw,
    wbraw,
    gsrc,
    wb0,
    grid_b,
    wb_all,
    tb,
    ta,
    prh,
    pool,
    pool2,
    pcat,
    gpo,
    gpc,
    gp,
    actt,
    act3,
    racc,
    out_v,
    gwb,
    rb1,
    rb2,
    sb,
    fin,
    gwa,
    ra1,
    ra2,
    ra3,
    sa,
    sin,
    s1,
    r1,
    sf,
    rf,
    sw,
    rw,
    sx,
    spool,
    rpool,
    sp,
    rp,
    sc,
    rc,
    sb1,
    qb1,
    sb2,
    qb2,
    sb3,
    qb3,
    sa1,
    qa1,
    sa2,
    qa2,
    sa3,
    qa3,
):
    f = lax.axis_index("filt")
    p = lax.axis_index("space")
    ns = lax.axis_size("space")
    xy = p // 2
    zl = p % 2
    me2 = f * 2 + zl

    def fmod(v):
        return lax.rem(v + NF, NF)

    def smod(v):
        return lax.rem(v + ns, ns)

    def xymod(v):
        return lax.rem(v + NXY, NXY)

    def send(src, dst, ss, rs, tf, tp):
        pltpu.make_async_remote_copy(
            src_ref=src,
            dst_ref=dst,
            send_sem=ss,
            recv_sem=rs,
            device_id={"filt": tf, "space": tp},
            device_id_type=pl.DeviceIdType.MESH,
        ).start()

    def wait(ref, sem):
        pltpu.make_async_copy(ref, ref, sem).wait()

    barrier = pltpu.get_barrier_semaphore()

    def greet(tf, tp):
        pl.semaphore_signal(
            barrier,
            inc=1,
            device_id={"filt": tf, "space": tp},
            device_id_type=pl.DeviceIdType.MESH,
        )

    cross = xymod(xy + 2 * zl - 1) * 2 + 1 - zl
    greet(f, cross)
    greet(fmod(f - 1), cross)
    greet(fmod(f + 1), cross)
    greet(fmod(f - 1), xymod(xy + 1) * 2 + zl)
    greet(fmod(f + 1), xymod(xy - 1) * 2 + zl)

    @pl.loop(1, NXY)
    def _(j):
        t = xymod(me2 + j)
        greet(t // 2, xy * 2 + lax.rem(t, 2))

    @pl.loop(1, NXY)
    def _(j):
        greet(f, xymod(xy + j) * 2 + zl)

    loads = [
        pltpu.make_async_copy(src, dst, sin.at[n])
        for n, (src, dst) in enumerate(
            ((gout_h, graw), (wb_h, wbraw), (pre_h, praw), (wa_h, waraw), (act_h, araw))
        )
    ]
    for load in loads:
        load.start()

    def selection(rows, per, high, low):
        row = lax.broadcasted_iota(jnp.int32, (rows, 4 * high), 0)
        col = lax.broadcasted_iota(jnp.int32, (rows, 4 * high), 1)
        tap = lax.shift_right_logical(row, per.bit_length() - 1)
        dx = lax.shift_right_logical(tap * 11, 5)
        dy = tap - 3 * dx
        place = (2 - dx) * high + (2 - dy) * low + (row - tap * per)
        return jnp.where(col == place, 1.0, 0.0).astype(BF)

    def arranged(raw, per, high, low):
        place = selection(9 * per, per, high, low)
        parts = []
        for dz in range(3):
            tall = jnp.concatenate([raw[3 * k + dz].astype(F32) for k in range(9)], axis=0)
            parts.append(
                lax.dot_general(
                    tall.astype(BF),
                    place,
                    (((0,), (0,)), ((), ())),
                    preferred_element_type=F32,
                )
            )
        return jnp.concatenate(parts, axis=0)

    loads[0].wait()
    rows = jnp.swapaxes(graw[...].astype(F32), 0, 1).reshape(512, 128)
    edge = jnp.zeros((8, 128), F32)
    gsrc[...] = jnp.concatenate([edge, rows, edge], axis=0).astype(BF)
    loads[1].wait()
    wb0[...] = arranged(wbraw, 8, 32, 8).astype(BF)

    pl.semaphore_wait(barrier, 2 * (NXY - 1) + 5)

    core = lax.rem(f, 2)
    sibling = f + 1 - 2 * core

    toward = fmod(f + 4 * zl - 2)
    send(wb0, wb_all.at[f], sw.at[1], rw.at[f], fmod(f + 4), xy * 2 + 1 - zl)
    send(wb0, wb_all.at[f], sw.at[2], rw.at[f], toward, p)
    send(wb0, wb_all.at[f], sw.at[3], rw.at[f], toward, xy * 2 + 1 - zl)

    send(wb0, wb_all.at[f], sx.at[0], rw.at[f], sibling, p)
    wb_all[f] = wb0[...]

    def block(t):
        return gsrc.at[pl.ds(pl.multiple_of(t * 32, 16), 48)]

    @pl.loop(1, NXY)
    def _(j):
        t = xymod(me2 + j)
        send(
            block(t),
            grid_b.at[f, 1 + zl],
            s1.at[j],
            r1.at[me2],
            t // 2,
            xy * 2 + lax.rem(t, 2),
        )

    loads[2].wait()
    for x in range(2):
        turned = jnp.swapaxes(praw[:, x].astype(F32), 0, 1)
        prh[1 + x, 1:17] = turned.astype(BF)

    pre_moves = (
        (prh.at[1, pl.ds(1, 16)], prh.at[3, pl.ds(1, 16)], 0, -1),
        (prh.at[2, pl.ds(1, 16)], prh.at[0, pl.ds(1, 16)], 0, 1),
        (prh.at[pl.ds(1, 2), 1], prh.at[pl.ds(1, 2), 17], -1, 0),
        (prh.at[pl.ds(1, 2), 16], prh.at[pl.ds(1, 2), 0], 1, 0),
        (prh.at[1, 1], prh.at[3, 17], -1, -1),
        (prh.at[1, 16], prh.at[3, 0], 1, -1),
        (prh.at[2, 1], prh.at[0, 17], -1, 1),
        (prh.at[2, 16], prh.at[0, 0], 1, 1),
    )

    grid_b[f, 1 + zl] = gsrc[pl.ds(pl.multiple_of(me2 * 32, 16), 48)]

    def forward(s):
        sz = lax.rem(s, 2)
        send(
            grid_b.at[s // 2, 1 + sz],
            grid_b.at[s // 2, 3 - 3 * sz],
            sf.at[s],
            rf.at[s],
            f,
            xymod(xy + 2 * sz - 1) * 2 + zl,
        )

    forward(me2)

    fine_row = lax.broadcasted_iota(jnp.int32, (256, 128), 0)
    fine_col = lax.broadcasted_iota(jnp.int32, (256, 128), 1)
    down = jnp.where(lax.shift_right_logical(fine_row, 1) == fine_col, 1.0, 0.0).astype(BF)
    total = jnp.zeros((ROWS * 32, 128), F32)
    for x2 in range(2):
        relu = jnp.maximum(prh[1 + x2, 1:17], jnp.zeros((), BF)).reshape(ROWS, 2, 32, 256)
        for y2 in range(2):
            total += jnp.dot(
                relu[:, y2].reshape(ROWS * 32, 256), down, preferred_element_type=F32
            )
    pool[...] = (total * 0.125).astype(BF).reshape(ROWS, 32, 128)
    send(
        pool.at[pl.ds(4 - 4 * zl, 4)],
        pool2.at[zl],
        spool.at[0],
        rpool.at[0],
        f,
        xy * 2 + 1 - zl,
    )
    pool2[zl] = pool[pl.ds(4 * zl, 4)]

    for n, (src, dst, df, dp) in enumerate(pre_moves):
        send(src, dst, sp.at[n], rp.at[n], fmod(f + df), smod(p + dp))

    for j in (1, 3, 2):
        s = fmod(f - 2 * j)
        wait(wb0, rw.at[s])
        send(wb_all.at[s], wb_all.at[s], sx.at[j], rw.at[s], sibling, p)

    @pl.loop(1, NXY)
    def _(j):
        s = xymod(me2 - j)
        wait(grid_b.at[0, 0], r1.at[s])
        forward(s)


    @pl.loop(0, 4)
    def _(j):
        wait(wb0, rw.at[2 * j + 1 - core])

    for n in range(NF):
        wide_b = wb_all[n].astype(F32)
        for k, turn in enumerate((0, 8, 32, 40)):
            tb[k * 96 : k * 96 + 96, n * 128 : n * 128 + 128] = (
                pltpu.roll(wide_b, turn, 1) if turn else wide_b
            ).astype(BF)

    @pl.loop(0, NXY)
    def _(j):
        wait(grid_b.at[0, 0], rf.at[j])

    @pl.when(xy == 0)
    def _():
        grid_b[:, 0] = jnp.zeros((NF,) + grid_b.shape[2:], BF)

    @pl.when(xy == NXY - 1)
    def _():
        grid_b[:, 3] = jnp.zeros((NF,) + grid_b.shape[2:], BF)

    g_cat = jnp.concatenate(
        [grid_b[:, :, 16 * b : 16 * b + 32, :].reshape(1024, 128) for b in range(2)], axis=1
    )
    prod = jnp.dot(tb[...], g_cat, preferred_element_type=F32)
    for b in range(2):
        term = prod[:, b * 128 : b * 128 + 128].reshape(2, 2, 3, 32, 128)
        rows = term[:, :, 1] + shifted(term[:, :, 0], -1) + shifted(term[:, :, 2], 1)
        gpo[:, 2 * b : 2 * b + 2] = rows.astype(BF)

    right = xymod(xy + 1) * 2
    left = xymod(xy - 1) * 2 + 1
    step = fmod(f + 2 * zl - 1)
    own_rows = pl.ds(1 + 4 * zl, 4)
    far = 9 - 9 * zl
    both = pl.ds(0, 2)
    coarse_moves = (
        (gpo, gpc.at[pl.ds(zl, 2), own_rows], 0, f, xy * 2 + 1 - zl),
        (gpo.at[1], gpc.at[0, own_rows], 1 + zl, f, right),
        (gpo.at[0], gpc.at[2, own_rows], 1 + zl, f, left),
        (gpo.at[both, 3 * zl], gpc.at[pl.ds(1, 2), far], 3 + zl, step, xy * 2),
        (gpo.at[both, 3 * zl], gpc.at[pl.ds(0, 2), far], 3 + zl, step, xy * 2 + 1),
        (gpo.at[1, 3 * zl], gpc.at[0, far], 5 + zl, step, right),
        (gpo.at[0, 3 * zl], gpc.at[2, far], 5 + zl, step, left),
    )
    for n, (src, dst, slot, tf, tp) in enumerate(coarse_moves):
        send(src, dst, sc.at[n], rc.at[slot], tf, tp)
    gpc[pl.ds(1 - zl, 2), own_rows] = gpo[...]

    wait(pool2.at[0], rpool.at[0])
    mid = pool2[...].reshape(256, 128).astype(F32)
    for k, version in enumerate((shifted(mid, 1), mid, shifted(mid, -1), jnp.zeros_like(mid))):
        version = version.astype(BF).reshape(2, 2, 2, 32, 128)
        for x2 in range(2):
            for b in range(2):
                for y2 in range(2):
                    r0 = (x2 * 2 + y2) * 128 + k * 32
                    pcat[r0 : r0 + 32, b * 128 : b * 128 + 128] = version[x2, b, y2]
    pairs = lax.dot_general(
        g_cat, pcat[...], (((1,), (1,)), ((), ())), preferred_element_type=F32
    ).reshape(NF, 4, 4, 8, 512)
    folded = None
    for x2 in range(2):
        for y2 in range(2):
            c0 = (x2 * 2 + y2) * 128
            term = pairs[:, x2 : x2 + 3, y2 : y2 + 3, :, c0 : c0 + 128]
            folded = term if folded is None else folded + term
    folded = jnp.concatenate(
        [folded.reshape(NF, 72, 128), jnp.zeros((NF, 24, 128), F32)], axis=1
    )
    gwb[...] = folded.astype(BF).reshape(2 * NF, 48, 128)

    @pl.loop(1, NXY)
    def _(j):
        k = xymod(xy + j)
        send(gwb.at[k], rb1.at[xy], sb1.at[j], qb1.at[xy], f, k * 2 + zl)

    rb1[xy] = gwb[xy]

    loads[4].wait()
    for x in range(2):
        actt[x] = jnp.swapaxes(araw[:, x].astype(F32), 0, 1)

    for b in range(8):
        for x2 in range(2):
            for y2 in range(2):
                wide = actt[x2, 2 * b + y2]
                r0, c0 = (x2 * 2 + y2) * 128, b * 256
                act3[r0 : r0 + 32, c0 : c0 + 256] = shifted(wide, 1).astype(BF)
                act3[r0 + 32 : r0 + 64, c0 : c0 + 256] = wide.astype(BF)
                act3[r0 + 64 : r0 + 96, c0 : c0 + 256] = shifted(wide, -1).astype(BF)
                act3[r0 + 96 : r0 + 128, c0 : c0 + 256] = jnp.zeros((32, 256), BF)

    wait(gpo, rc.at[0])
    for n in range(2):
        wait(gpo.at[0], rc.at[1 + n])
        wait(gpo.at[both, 0], rc.at[3 + n])
        wait(gpo.at[0, 0], rc.at[5 + n])
    for n, (src, dst, df, dp) in enumerate(pre_moves):
        wait(dst, rp.at[n])

    @pl.when(p == 0)
    def _():
        prh[0] = jnp.zeros(prh.shape[1:], BF)

    @pl.when(p == ns - 1)
    def _():
        prh[3] = jnp.zeros(prh.shape[1:], BF)

    @pl.when(f == 0)
    def _():
        prh[:, 0] = jnp.zeros((4, 32, 256), BF)

    @pl.when(f == NF - 1)
    def _():
        prh[:, 17] = jnp.zeros((4, 32, 256), BF)

    up_row = lax.broadcasted_iota(jnp.int32, (128, 256), 0)
    up_col = lax.broadcasted_iota(jnp.int32, (128, 256), 1)
    up = jnp.where(lax.shift_right_logical(up_col, 1) == up_row, 0.125, 0.0).astype(BF)
    for plane in range(3):
        fine = (
            jnp.dot(gpc[plane].reshape(320, 128), up, preferred_element_type=F32)
            .astype(BF)
            .reshape(10, 32, 256)
        )
        for xh in ((0,), (1, 2), (3,))[plane]:
            for row in range(10):
                for yh in (2 * row - 1, 2 * row):
                    if 0 <= yh <= 17:
                        gp[xh, yh] = jnp.where(
                            prh[xh, yh] > jnp.zeros((), BF), fine[row], jnp.zeros((), BF)
                        )

    cells = jnp.concatenate(
        [gp[:, 2 * b : 2 * b + 4].reshape(512, 256) for b in range(8)], axis=1
    )
    for x2 in range(2):
        r0, c0 = 128 * x2, 256 * x2
        racc[r0 : r0 + 384, c0 : c0 + 256] = lax.dot_general(
            cells[r0 : r0 + 384],
            act3[c0 : c0 + 256],
            (((1,), (1,)), ((), ())),
            preferred_element_type=F32,
        )

    taps = []
    for dx in range(3):
        for dy in range(3):
            term = None
            for x2 in range(2):
                for y2 in range(2):
                    r0 = ((x2 + dx) * 4 + y2 + dy) * 32
                    c0 = (x2 * 2 + y2) * 128
                    piece = racc[r0 : r0 + 32, c0 : c0 + 128]
                    term = piece if term is None else term + piece
            taps.append(term)
    full = jnp.concatenate(taps, axis=0)
    rest = full[216:288]
    tail = jnp.concatenate([pltpu.roll(rest, turn, 1) for turn in (96, 64, 32)], axis=0)
    lane = lax.broadcasted_iota(jnp.int32, (216, 128), 1)
    packed = jnp.where(lane < 96, full[:216], tail)
    packed = jnp.concatenate([packed, jnp.zeros((40, 128), F32)], axis=0)
    gwa[...] = packed.astype(BF).reshape(NXY, 16, 128)

    for j in FAR_XY:
        k = xymod(xy + j)
        send(gwa.at[k], ra1.at[xy], sa1.at[j], qa1.at[xy], f, k * 2 + zl)

    ra1[xy] = gwa[xy]

    @pl.loop(1, NXY)
    def _(j):
        wait(rb1.at[0], qb1.at[xymod(xy + j)])

    owner = xy // 2
    sb[...] = jnp.sum(rb1[...].astype(F32), axis=0).astype(BF)
    for zt in range(2):

        @pl.when((f != owner) | (zl != zt))
        def _():
            send(sb, rb2.at[me2], sb2.at[zt], qb2.at[me2], owner, xy * 2 + zt)

    loads[3].wait()
    wide_a = arranged(waraw, 32, 128, 32)
    for n, turn in enumerate((0, 32, 128, 160)):
        ta[n * 96 : n * 96 + 96] = (
            pltpu.roll(wide_a, turn, 1) if turn else wide_a
        ).astype(BF)

    for b in range(8):
        cells = gp[:, 2 * b : 2 * b + 4].reshape(512, 256)
        term = jnp.dot(ta[...], cells, preferred_element_type=F32).reshape(2, 2, 3, 32, 256)
        rows = term[:, :, 1] + shifted(term[:, :, 0], -1) + shifted(term[:, :, 2], 1)
        out_v[:, 2 * b : 2 * b + 2] = rows.astype(BF)

    for x in range(2):
        turned = jnp.swapaxes(out_v[x].astype(F32), 0, 1)
        out_t[:, x] = turned.astype(BF)


    @pl.loop(1, NXY)
    def _(j):
        wait(ra1.at[0], qa1.at[xymod(xy + j)])

    sa[...] = jnp.sum(ra1[...].astype(F32), axis=0).astype(BF)

    for j in FAR_Z:
        t = xymod(me2 + j)
        send(sa, ra2.at[me2], sa2.at[j], qa2.at[me2], t // 2, xy * 2 + lax.rem(t, 2))

    ra2[me2] = sa[...]

    half = lax.rem(xy, 2)

    @pl.when(f == owner)
    def _():
        rb2[me2] = sb[...]

        @pl.loop(1, NXY)
        def _(j):
            wait(rb2.at[0], qb2.at[xymod(me2 + j)])

        fin[half] = jnp.sum(rb2[...].astype(F32), axis=0)

        @pl.loop(1, NXY)
        def _(j):
            send(fin.at[half], fin.at[half], sb3.at[j], qb3.at[half], f, xymod(xy + j) * 2 + zl)

    @pl.loop(1, NXY)
    def _(j):
        wait(ra2.at[0], qa2.at[xymod(me2 + j)])

    ra3[xy] = jnp.sum(ra2[...].astype(F32), axis=0).astype(BF)

    for j in FAR_XY:
        k = xymod(xy + j)
        send(ra3.at[xy], ra3.at[xy], sa3.at[j], qa3.at[xy], f, k * 2 + zl)

    for h in range(2):

        @pl.when(xy != 2 * f + h)
        def _():
            wait(fin.at[h], qb3.at[h])

    scale_b = 1.0 / math.sqrt(ns * NF * ROWS * 128)
    scale_a = 1.0 / math.sqrt(8 * ns * NF * ROWS * 128)

    def unfold(full, per, target, scale):
        for dx in range(3):
            for dy in range(3):
                r0 = ((2 - dx) * 3 + 2 - dy) * per
                for dz in range(3):
                    target[9 * dx + 3 * dy + dz] = (
                        full[r0 : r0 + per, dz * 32 : dz * 32 + 32] * scale
                    )

    unfold(fin[...].reshape(96, 128), 8, gwb_out, scale_b)

    @pl.loop(1, NXY)
    def _(j):
        wait(grid_b.at[0, 0], s1.at[j])
        wait(gwb.at[0], sb1.at[j])
        wait(gwa.at[0], sa1.at[j])
        wait(sa, sa2.at[j])

    @pl.loop(0, NXY)
    def _(j):
        wait(grid_b.at[0, 0], sf.at[j])

    @pl.loop(1, 4)
    def _(j):
        wait(wb0, sw.at[j])

    @pl.loop(0, 4)
    def _(j):
        wait(wb0, sx.at[j])

    wait(pool2.at[0], spool.at[0])
    for n, (src, dst, df, dp) in enumerate(pre_moves):
        wait(src, sp.at[n])
    for n, (src, dst, slot, tf, tp) in enumerate(coarse_moves):
        wait(src, sc.at[n])

    for zt in range(2):

        @pl.when((f != owner) | (zl != zt))
        def _():
            wait(sb, sb2.at[zt])

    @pl.when(f == owner)
    def _():
        @pl.loop(1, NXY)
        def _(j):
            wait(fin.at[0], sb3.at[j])


    @pl.loop(1, NXY)
    def _(j):
        wait(ra3.at[0], qa3.at[xymod(xy + j)])

    packed = ra3[...].astype(F32).reshape(256, 128)
    rest = None
    lane = lax.broadcasted_iota(jnp.int32, (72, 128), 1)
    for n in range(3):
        piece = pltpu.roll(packed[n * 72 : n * 72 + 72], 32 * (n + 1), 1)
        rest = piece if n == 0 else jnp.where(lane < 32 * n, rest, piece)
    full = jnp.concatenate([packed[:216], rest], axis=0)
    unfold(full, 32, gwa_out, scale_a)

    @pl.loop(1, NXY)
    def _(j):
        wait(ra3.at[0], sa3.at[j])


def per_device(activation, preact, grad_out, weight_a, weight_b):
    hbm = pl.BlockSpec(memory_space=pltpu.HBM)
    vmem = pl.BlockSpec(memory_space=pltpu.VMEM)
    dma = pltpu.SemaphoreType.DMA
    out, gwa, gwb = pl.pallas_call(
        kernel,
        out_shape=(
            jax.ShapeDtypeStruct((32, 2, 16, 256), BF),
            jax.ShapeDtypeStruct((27, 32, 32), F32),
            jax.ShapeDtypeStruct((27, 8, 32), F32),
        ),
        in_specs=[hbm] * 5,
        out_specs=(vmem,) * 3,
        scratch_shapes=[
            pltpu.VMEM((8, 64, 128), BF),
            pltpu.VMEM((32, 2, 16, 256), BF),
            pltpu.VMEM((32, 2, 16, 256), BF),
            pltpu.VMEM((27, 32, 32), BF),
            pltpu.VMEM((27, 8, 32), BF),
            pltpu.VMEM((528, 128), BF),
            pltpu.VMEM((96, 128), BF),
            pltpu.VMEM((NF, 4, 48, 128), BF),
            pltpu.VMEM((NF, 96, 128), BF),
            pltpu.VMEM((384, 1024), BF),
            pltpu.VMEM((384, 512), BF),
            pltpu.VMEM((4, 18, 32, 256), BF),
            pltpu.VMEM((ROWS, 32, 128), BF),
            pltpu.VMEM((2, 4, 32, 128), BF),
            pltpu.VMEM((512, 256), BF),
            pltpu.VMEM((2, 4, 32, 128), BF),
            pltpu.VMEM((3, 10, 32, 128), BF),
            pltpu.VMEM((4, 18, 32, 256), BF),
            pltpu.VMEM((2, 16, 32, 256), F32),
            pltpu.VMEM((512, 2048), BF),
            pltpu.VMEM((512, 512), F32),
            pltpu.VMEM((2, 16, 32, 256), BF),
            pltpu.VMEM((NXY, 48, 128), BF),
            pltpu.VMEM((NXY, 48, 128), BF),
            pltpu.VMEM((NXY, 48, 128), BF),
            pltpu.VMEM((48, 128), BF),
            pltpu.VMEM((2, 48, 128), F32),
            pltpu.VMEM((NXY, 16, 128), BF),
            pltpu.VMEM((NXY, 16, 128), BF),
            pltpu.VMEM((NXY, 16, 128), BF),
            pltpu.VMEM((NXY, 16, 128), BF),
            pltpu.VMEM((16, 128), BF),
            dma((5,)),
            dma((NXY,)),
            dma((NXY,)),
            dma((NXY,)),
            dma((NXY,)),
            dma((NF,)),
            dma((NF,)),
            dma((4,)),
            dma((1,)),
            dma((1,)),
            dma((8,)),
            dma((8,)),
            dma((7,)),
            dma((7,)),
            dma((NXY,)),
            dma((NXY,)),
            dma((2,)),
            dma((NXY,)),
            dma((NXY,)),
            dma((2,)),
            dma((NXY,)),
            dma((NXY,)),
            dma((NXY,)),
            dma((NXY,)),
            dma((NXY,)),
            dma((NXY,)),
        ],
        compiler_params=pltpu.CompilerParams(
            collective_id=0, has_side_effects=True, vmem_limit_bytes=32 * 1024 * 1024
        ),
    )(
        *(
            pltpu.with_memory_space_constraint(x, pltpu.HBM)
            for x in (grad_out.reshape(8, 64, 128), preact, activation, weight_a, weight_b)
        )
    )
    return (out, gwa, gwb)


def solution(mesh):
    placed = (
        P(None, "space", "filt", None),
        P(None, "space", "filt", None),
        P("filt", "space", None, None),
        P(),
        P(None, "filt", None),
    )
    return jax.shard_map(
        per_device,
        mesh=mesh,
        in_specs=placed,
        out_specs=(P(None, "space", "filt", None), P(), P(None, "filt", None)),
        check_vma=False,
    )
```
